32 devices in a mesh: dp: 8 (over y, x, core), etp: 4 (over z).
Axes of the slice: x: 2, y: 2, z: 4, core: 2. Of those that a mesh axis runs over, the one named last changes fastest.
Arguments:
- tokens: bfloat16 [2048, 3072], P('dp'), may hold values from -6 to 6
- cotangent: bfloat16 [2048, 3072], P('dp'), may hold values from -6 to 6
- w_gate: float32 [2, 3072, 6144], P(None, 'dp', 'etp'), may hold values from -0.109375 to 0.109375
- w_up: float32 [2, 3072, 6144], P(None, 'dp', 'etp'), may hold values from -0.109375 to 0.109375
- w_down: float32 [2, 6144, 3072], P(None, 'etp', 'dp'), may hold values from -0.078125 to 0.078125
- slot_token: int32 [4096], P('dp'), may hold values from 0 to 255, as said below
- slot_gate: int32 [4096], P('dp'), may hold values from 0 to 16
- block_expert: int32 [32], P('dp'), may hold values from 0 to 2, as said below
Outputs:
- combined: bfloat16 [2048, 3072], P('dp', 'etp')
- input_grad: bfloat16 [2048, 3072], P('dp', 'etp')
The draws below stay inside these ranges and needn't reach their ends.
Inputs may be any that keep to these rules, and one draw needn't show every extreme that they name: `slot_token`: within the live blocks of one expert on one dp index no token repeats, so each expert has at most 2 live blocks there. `block_expert`: blocks of the experts and padding blocks stand in any order; each expert has at most 2 blocks on one dp index, and on some dp index every block is live.
All inputs are finite; a program needn't handle non-finite values.
Results may differ from the reference program's by a relative error of at most 0.014.
Values may be sent and summed in bfloat16 or wider, within the bound.
No kernel may reach another device: no remote copies, remote signals or barrier semaphores. Data moves between devices by JAX's collectives and lax.ppermute only.
A program may use at most 128 MiB of HBM per device.

```python
import jax
import jax.numpy as jnp
from jax import lax

D = 3072
FF = 6144
E = 2
BLOCK = 128
TOK_DEV = 256
BLOCKS_DEV = 4
TOKENS = 2048
BLOCKS = 32
SLOTS = 4096
N_DP = 8
N_ETP = 4


def routing_tables(key):
    per_expert = TOK_DEV // BLOCK
    count_key, pick_key, order_key, token_key = jax.random.split(jax.random.fold_in(key, 7), 4)
    counts = jax.random.randint(count_key, (N_DP, 2), 0, per_expert + 1, dtype=jnp.int32)
    full_rank = jax.random.randint(pick_key, (), 0, N_DP, dtype=jnp.int32)
    rank_ids = jnp.arange(N_DP, dtype=jnp.int32)
    counts = jnp.where((rank_ids == full_rank)[:, None], per_expert, counts)
    positions = jnp.arange(BLOCKS_DEV, dtype=jnp.int32)[None, :]
    first = counts[:, :1]
    second = counts[:, 1:]
    labels = jnp.where(positions < first, 0, jnp.where(positions < first + second, 1, 2)).astype(jnp.int32)
    within = jnp.where(labels == 0, positions, jnp.where(labels == 1, positions - first, 0)).astype(jnp.int32)
    order_keys = jax.random.split(order_key, N_DP)
    orders = jax.vmap(lambda subkey: jax.random.permutation(subkey, BLOCKS_DEV))(order_keys).astype(jnp.int32)
    inverse = jnp.argsort(orders, axis=1, stable=True)
    block_labels = jnp.take_along_axis(labels, inverse, axis=1)
    block_within = jnp.take_along_axis(within, inverse, axis=1)
    token_keys = jax.random.split(token_key, N_DP * 2)
    shuffles = jax.vmap(lambda subkey: jax.random.permutation(subkey, TOK_DEV))(token_keys).astype(jnp.int32)
    shuffles = shuffles.reshape(N_DP, 2, per_expert, BLOCK)
    expert_pick = jnp.minimum(block_labels, 1)
    slot_tokens = shuffles[rank_ids[:, None], expert_pick, block_within]
    expert_ids = jnp.where(block_labels == 2, E, block_labels).astype(jnp.int32)
    return (slot_tokens.reshape(SLOTS).astype(jnp.int32), expert_ids.reshape(BLOCKS).astype(jnp.int32))


def draw_slot_token(key, part):
    return routing_tables(key)[0]


def draw_block_expert(key, part):
    return routing_tables(key)[1]


def place_ends(values, stream_key, least, top_value):
    longest = values.shape.index(max(values.shape))
    spots = []
    for shift in (0, 1):
        where = [jax.random.randint(jax.random.fold_in(stream_key, axis), (), 0, length) for axis, length in enumerate(values.shape)]
        where[longest] = (where[longest] + shift) % values.shape[longest]
        spots.append(tuple(where))
    return values.at[spots[0]].set(least).at[spots[1]].set(top_value)


def block_levels(key, shape, pieces, least, largest):
    level = 1.0
    for axis_at, shards_of in pieces:
        steps = jax.random.uniform(jax.random.fold_in(jax.random.fold_in(key, 6), axis_at), (shards_of,), jnp.float32, least / len(pieces), largest / len(pieces))
        level = level * jnp.repeat(jnp.exp(steps), shape[axis_at] // shards_of).reshape((-1,) + (1,) * (len(shape) - 1 - axis_at))
    return level


def normal_values(key, dims, width, bound, shards=(), kind=jnp.bfloat16):
    drawn = jax.random.normal(key, dims, jnp.float32) * width
    if len(shards) > 0:
        drawn = block_levels(key, dims, shards, -0.22, 0.18) * drawn
    return jnp.clip(drawn, min=-bound, max=bound).astype(kind)


def setup_inputs(seed: int = 0) -> dict:
    splits = jax.random.split(jax.random.key(seed), 9)
    return {
        "tokens": normal_values(splits[0], (TOKENS, D), 1.0, 6.0, ((0, 8),)),
        "cotangent": normal_values(splits[1], (TOKENS, D), 1.0, 6.0, ((0, 8),)),
        "w_gate": normal_values(splits[2], (E, D, FF), D ** -0.5, 0.109375, ((1, 8), (2, 4)), jnp.float32),
        "w_up": normal_values(splits[3], (E, D, FF), D ** -0.5, 0.109375, ((1, 8), (2, 4)), jnp.float32),
        "w_down": normal_values(splits[4], (E, FF, D), FF ** -0.5, 0.078125, ((1, 4), (2, 8)), jnp.float32),
        "slot_token": draw_slot_token(jax.random.fold_in(splits[8], 71), 0),
        "slot_gate": place_ends(jax.random.randint(splits[6], (SLOTS,), 0, 17), jax.random.fold_in(splits[6], 1), 0, 16).astype(jnp.int32),
        "block_expert": draw_block_expert(jax.random.fold_in(splits[8], 71), 0),
    }


gate_steps = 16.0


def reference(tokens, cotangent, w_gate, w_up, w_down, slot_token, slot_gate, block_expert):
    gate_low = w_gate.astype(jnp.bfloat16)
    up_low = w_up.astype(jnp.bfloat16)
    down_low = w_down.astype(jnp.bfloat16)
    experts_count = w_gate.shape[0]
    group_width = FF // N_ETP
    scale = slot_gate.astype(jnp.float32) / gate_steps

    def one_rank(rank_index):
        token_base = rank_index * TOK_DEV
        own_tokens = lax.dynamic_slice_in_dim(tokens, token_base, TOK_DEV, 0)
        own_cotangent = lax.dynamic_slice_in_dim(cotangent, token_base, TOK_DEV, 0)
        zeroed = jnp.zeros((N_ETP, TOK_DEV, D), jnp.float32)

        def step(totals, block_index):
            block_id = rank_index * BLOCKS_DEV + block_index
            expert = block_expert[block_id]

            def compute_block(state):
                y_total, dx_total = state
                chosen = jnp.minimum(expert, experts_count - 1)
                token_rows = lax.dynamic_slice_in_dim(slot_token, block_id * BLOCK, BLOCK, 0)
                gate_scale = lax.dynamic_slice_in_dim(scale, block_id * BLOCK, BLOCK, 0)[:, None]
                gate_mat = gate_low[chosen]
                up_mat = up_low[chosen]
                down_mat = down_low[chosen]
                inputs = own_tokens[token_rows]
                upstream = own_cotangent[token_rows]
                gate_pre = jnp.dot(inputs, gate_mat, preferred_element_type=jnp.float32)
                up_pre = jnp.dot(inputs, up_mat, preferred_element_type=jnp.float32)
                squash = jax.nn.sigmoid(gate_pre)
                active = gate_pre * squash
                hidden = (active * up_pre).astype(jnp.bfloat16)
                d_out = (gate_scale * upstream.astype(jnp.float32)).astype(jnp.bfloat16)
                d_hidden = jnp.dot(d_out, down_mat.T, preferred_element_type=jnp.float32)
                d_pre = (d_hidden * up_pre * squash * (1.0 + gate_pre * (1.0 - squash))).astype(jnp.bfloat16)
                d_up = (d_hidden * active).astype(jnp.bfloat16)
                produced_list = []
                backward_list = []
                for group in range(N_ETP):
                    columns = slice(group * group_width, (group + 1) * group_width)
                    produced = jnp.dot(hidden[:, columns], down_mat[columns], preferred_element_type=jnp.float32)
                    produced_list.append(produced * gate_scale)
                    backward = jnp.dot(d_pre[:, columns], gate_mat[:, columns].T, preferred_element_type=jnp.float32)
                    backward = backward + jnp.dot(d_up[:, columns], up_mat[:, columns].T, preferred_element_type=jnp.float32)
                    backward_list.append(backward)
                y_total = y_total.at[:, token_rows].add(jnp.stack(produced_list))
                dx_total = dx_total.at[:, token_rows].add(jnp.stack(backward_list))
                return y_total, dx_total

            def skip_block(state):
                return state

            return lax.cond(expert < experts_count, compute_block, skip_block, totals), None

        (y_total, dx_total), _ = lax.scan(step, (zeroed, zeroed), jnp.arange(BLOCKS_DEV, dtype=jnp.int32))
        y_low = lax.optimization_barrier(y_total.astype(jnp.bfloat16))
        dx_low = lax.optimization_barrier(dx_total.astype(jnp.bfloat16))
        combined_rows = jnp.sum(y_low.astype(jnp.float32), axis=0).astype(jnp.bfloat16)
        grad_rows = jnp.sum(dx_low.astype(jnp.float32), axis=0).astype(jnp.bfloat16)
        return combined_rows, grad_rows

    combined, input_grad = lax.map(one_rank, jnp.arange(N_DP, dtype=jnp.int32))
    return combined.reshape(TOKENS, D), input_grad.reshape(TOKENS, D)
```

```python
import functools

import jax
import jax.numpy as jnp
from jax import lax
from jax.experimental import pallas as pl
from jax.experimental.pallas import tpu as pltpu
from jax.sharding import PartitionSpec as P

gate_steps = 16.0
vmem_limit = 48 * 1024 * 1024
shares = 4


def swap(value, mask, size):
    return lax.ppermute(value, "dp", [(i, i ^ mask) for i in range(size)])


def steps_of(rows):
    return max(step for step in (1, 2, 4) if rows % (16 * step) == 0)


def cast_rows_kernel(pick_ref, gate_ref, up_ref, *out_refs):
    parts = shares // gate_ref.shape[0]
    width = out_refs[0].shape[-1]
    for share, out_ref in enumerate(out_refs):
        expert = pick_ref[share] // parts
        lanes = pl.ds(pl.multiple_of(pick_ref[share] % parts * width, 128), width)
        out_ref[0] = gate_ref[expert, :, lanes].astype(jnp.bfloat16)
        out_ref[1] = up_ref[expert, :, lanes].astype(jnp.bfloat16)


def cast_rows(pick, w_gate, w_up):
    experts, rows, hidden = w_gate.shape
    width = experts * hidden // shares
    steps = steps_of(rows)
    block = pl.BlockSpec((experts, rows // steps, hidden), lambda i, pick: (0, i, 0))
    return pl.pallas_call(
        cast_rows_kernel,
        grid_spec=pltpu.PrefetchScalarGridSpec(
            num_scalar_prefetch=1,
            grid=(steps,),
            in_specs=[block, block],
            out_specs=[pl.BlockSpec((2, rows // steps, width), lambda i, pick: (0, i, 0))] * shares,
        ),
        out_shape=[jax.ShapeDtypeStruct((2, rows, width), jnp.bfloat16)] * shares,
        compiler_params=pltpu.CompilerParams(vmem_limit_bytes=vmem_limit),
        name="cast_rows",
    )(pick, w_gate, w_up)


def cast_turned_kernel(pick_ref, down_ref, *out_refs):
    parts = shares // down_ref.shape[0]
    width = out_refs[0].shape[-1]
    for share, out_ref in enumerate(out_refs):
        expert = pick_ref[share] // parts
        rows = pl.ds(pl.multiple_of(pick_ref[share] % parts * width, 128), width)
        out_ref[...] = down_ref[expert, rows, :].T.astype(jnp.bfloat16)


def cast_turned(pick, w_down):
    experts, hidden, features = w_down.shape
    width = experts * hidden // shares
    tile = 128 if features % 128 == 0 else features
    return pl.pallas_call(
        cast_turned_kernel,
        grid_spec=pltpu.PrefetchScalarGridSpec(
            num_scalar_prefetch=1,
            grid=(features // tile,),
            in_specs=[pl.BlockSpec((experts, hidden, tile), lambda i, pick: (0, 0, i))],
            out_specs=[pl.BlockSpec((tile, width), lambda i, pick: (i, 0))] * shares,
        ),
        out_shape=[jax.ShapeDtypeStruct((features, width), jnp.bfloat16)] * shares,
        compiler_params=pltpu.CompilerParams(vmem_limit_bytes=vmem_limit),
        name="cast_turned",
    )(pick, w_down)


def token_scales(slot_token, slot_gate, block_expert, experts, token_count):
    block_rows = slot_token.shape[0] // block_expert.shape[0]
    scale = slot_gate.astype(jnp.float32) / gate_steps
    slot_expert = jnp.repeat(block_expert, block_rows)
    weight = jnp.where(slot_expert[None, :] == jnp.arange(experts)[:, None], scale[None, :], 0.0)
    hot = (slot_token[:, None] == jnp.arange(token_count)[None, :]).astype(jnp.bfloat16)
    return jnp.dot(weight.astype(jnp.bfloat16), hot, preferred_element_type=jnp.float32)


def shards(n, m, tokens, cotangent, w_gate, w_up, w_down, slot_token, slot_gate, block_expert):
    experts, rows, hidden = w_gate.shape
    width = experts * hidden // shares
    features = tokens.shape[1]
    count = tokens.shape[0]
    me = lax.axis_index("dp")
    top = n // 2
    masks = [0, 1, top, top + 1]
    gather_bits = [1 << i for i in range(1, n.bit_length() - 2)]
    mine = (me & 1) + 2 * (me // top)
    pick = jnp.stack([mine ^ share for share in range(shares)]).astype(jnp.int32)
    low, high = (((1,), (0,)), ((), ())), (((1,), (1,)), ((), ()))
    dot = functools.partial(lax.dot_general, preferred_element_type=jnp.float32)

    def spread(pieces):
        blocks = {masks[0]: pieces[0]}
        for share in range(1, shares):
            blocks[masks[share]] = swap(pieces[share], masks[share], n)
        for bit in gather_bits:
            for key in list(blocks):
                blocks[key ^ bit] = swap(blocks[key], bit, n)
        return blocks

    both = spread(cast_rows(pick, w_gate, w_up))
    turned = spread(cast_turned(pick, w_down))

    scale = token_scales(slot_token, slot_gate, block_expert, experts, count)

    def share_tokens(value):
        far = swap(value, top, n)
        pair = jnp.concatenate([value, far])
        near = swap(pair, 1, n)
        return jnp.concatenate([value, near[:count], far, near[count:]])

    x = share_tokens(tokens)
    u = share_tokens(cotangent)
    s = lax.dynamic_slice_in_dim(share_tokens(scale.T), mine // (shares // experts), 1, 1)

    full = jnp.zeros((2, features, width), jnp.bfloat16)
    for key, block in both.items():
        full = lax.dynamic_update_slice(full, block, (0, (me ^ key) * rows, 0))
    full_down = jnp.zeros((features, width), jnp.bfloat16)
    for key, block in turned.items():
        full_down = lax.dynamic_update_slice(full_down, block, ((me ^ key) * rows, 0))

    gate_pre = dot(x, full[0], low)
    up_pre = dot(x, full[1], low)
    squash = jax.nn.sigmoid(gate_pre)
    active = gate_pre * squash
    hid = (active * up_pre * s).astype(jnp.bfloat16)
    produced = dot(hid, full_down, high).astype(jnp.bfloat16)
    d_hidden = dot(u, full_down, low) * s
    d_pre = (d_hidden * up_pre * squash * (1.0 + gate_pre * (1.0 - squash))).astype(jnp.bfloat16)
    d_up = (d_hidden * active).astype(jnp.bfloat16)
    backward = (dot(d_pre, full[0], high) + dot(d_up, full[1], high)).astype(jnp.bfloat16)

    wide = jnp.float32

    def reduce(partial):
        parts = partial.reshape(shares, count, features)
        near = swap(jnp.stack([parts[1], parts[3]]), 1, n)
        own = parts[0].astype(wide) + near[0].astype(wide)
        other = (parts[2].astype(wide) + near[1].astype(wide)).astype(jnp.bfloat16)
        own = own + swap(other, top, n).astype(wide)
        z = lax.axis_index("etp")
        columns = features // m
        total = lax.dynamic_slice_in_dim(own, z * columns, columns, 1)
        low_own = own.astype(jnp.bfloat16)
        for step in range(1, m):
            target = lax.rem(z + step, m)
            part = lax.dynamic_slice_in_dim(low_own, target * columns, columns, 1)
            got = lax.ppermute(part, "etp", [(i, (i + step) % m) for i in range(m)])
            total = total + got.astype(wide)
        return total.astype(jnp.bfloat16)

    return reduce(produced), reduce(backward)


def solution(mesh):
    in_specs = (
        P("dp", None),
        P("dp", None),
        P(None, "dp", "etp"),
        P(None, "dp", "etp"),
        P(None, "etp", "dp"),
        P("dp"),
        P("dp"),
        P("dp"),
    )
    out_specs = (P("dp", "etp"), P("dp", "etp"))
    body = functools.partial(shards, mesh.shape["dp"], mesh.shape["etp"])
    return jax.shard_map(body, mesh=mesh, in_specs=in_specs, out_specs=out_specs, check_vma=False)
```

```python
import functools

import jax
import jax.numpy as jnp
from jax import lax
from jax.experimental import pallas as pl
from jax.experimental.pallas import tpu as pltpu
from jax.sharding import PartitionSpec as P

gate_steps = 16.0
vmem_limit = 48 * 1024 * 1024
shares = 4
slot_us = 5.0
flop_rate = 1_150_000_000
low, high = (((1,), (0,)), ((), ())), (((1,), (1,)), ((), ()))
dot = functools.partial(lax.dot_general, preferred_element_type=jnp.float32)
params = pltpu.CompilerParams(vmem_limit_bytes=vmem_limit)
anywhere = pl.BlockSpec(memory_space=pl.ANY)


def shape_of(value):
    return jax.ShapeDtypeStruct(value.shape, value.dtype)


class Clock:
    def __init__(self):
        self.token = blank((16, 128))

    def tick(self, release, wait=()):
        held = [self.token, *release]
        known = {id(value) for value in held}
        wait = [value for value in wait if id(value) not in known]
        self.token, *out = pl.pallas_call(
            lambda *refs: None,
            in_specs=[anywhere] * (len(held) + len(wait)),
            out_specs=[anywhere] * len(held),
            out_shape=[shape_of(value) for value in held],
            input_output_aliases={i: i for i in range(len(held))},
            cost_estimate=pl.CostEstimate(flops=int(slot_us * flop_rate), bytes_accessed=0, transcendentals=0),
            name="tick",
        )(*held, *wait)
        return out


def blank(shape):
    return pl.pallas_call(
        lambda *refs: None,
        out_specs=anywhere,
        out_shape=jax.ShapeDtypeStruct(shape, jnp.bfloat16),
        name="blank",
    )()


def swap(value, mask, size):
    return lax.ppermute(value, "dp", [(i, i ^ mask) for i in range(size)])


def steps_of(rows):
    return max(step for step in (1, 2, 4) if rows % (16 * step) == 0)


def cast_rows_kernel(pick_ref, gate_ref, up_ref, *out_refs):
    parts = shares // gate_ref.shape[0]
    width = out_refs[0].shape[-1]
    for share, out_ref in enumerate(out_refs):
        expert = pick_ref[share] // parts
        lanes = pl.ds(pl.multiple_of(pick_ref[share] % parts * width, 128), width)
        out_ref[0] = gate_ref[expert, :, lanes].astype(jnp.bfloat16)
        out_ref[1] = up_ref[expert, :, lanes].astype(jnp.bfloat16)


def cast_rows(pick, w_gate, w_up):
    experts, rows, hidden = w_gate.shape
    width = experts * hidden // shares
    steps = steps_of(rows)
    block = pl.BlockSpec((experts, rows // steps, hidden), lambda i, pick: (0, i, 0))
    return pl.pallas_call(
        cast_rows_kernel,
        grid_spec=pltpu.PrefetchScalarGridSpec(
            num_scalar_prefetch=1,
            grid=(steps,),
            in_specs=[block, block],
            out_specs=[pl.BlockSpec((2, rows // steps, width), lambda i, pick: (0, i, 0))] * shares,
        ),
        out_shape=[jax.ShapeDtypeStruct((2, rows, width), jnp.bfloat16)] * shares,
        compiler_params=params,
        name="cast_rows",
    )(pick, w_gate, w_up)


def cast_turned_kernel(pick_ref, down_ref, *refs):
    out_refs = refs[-shares:]
    parts = shares // down_ref.shape[0]
    width = out_refs[0].shape[-1]
    for share, out_ref in enumerate(out_refs):
        expert = pick_ref[share] // parts
        rows = pl.ds(pl.multiple_of(pick_ref[share] % parts * width, 128), width)
        out_ref[...] = down_ref[expert, rows, :].T.astype(jnp.bfloat16)


def cast_turned(pick, w_down, *earlier):
    experts, hidden, features = w_down.shape
    width = experts * hidden // shares
    tile = 128 if features % 128 == 0 else features
    return pl.pallas_call(
        cast_turned_kernel,
        grid_spec=pltpu.PrefetchScalarGridSpec(
            num_scalar_prefetch=1,
            grid=(features // tile,),
            in_specs=[pl.BlockSpec((experts, hidden, tile), lambda i, pick: (0, 0, i))]
            + [anywhere] * len(earlier),
            out_specs=[pl.BlockSpec((tile, width), lambda i, pick: (i, 0))] * shares,
        ),
        out_shape=[jax.ShapeDtypeStruct((features, width), jnp.bfloat16)] * shares,
        compiler_params=params,
        name="cast_turned",
    )(pick, w_down, *earlier)


def fetch(keys, refs, me, chunk, span, target, sems, start):
    rows = refs[0].shape[-2]
    per = span // rows
    for i, (key, ref) in enumerate(zip(keys, refs)):
        block = me ^ key

        @pl.when(block // per == chunk)
        def _(ref=ref, i=i, block=block):
            place = pl.ds(pl.multiple_of(block % per * rows, 16), rows)
            view = target.at[place] if len(target.shape) == 2 else target.at[:, place]
            copy = pltpu.make_async_copy(ref, view, sems.at[i])
            if start:
                copy.start()
            else:
                copy.wait()


def load(n, me, parts, blocks, x, weights, x_sems, sems):
    step = pl.program_id(0)
    copies = [pltpu.make_async_copy(part, x.at[i], x_sems.at[i]) for i, part in enumerate(parts)]

    @pl.when(step == 0)
    def _():
        fetch(range(n), blocks, me, 0, weights.shape[-2], weights, sems, True)
        for copy in copies:
            copy.start()
        fetch(range(n), blocks, me, 0, weights.shape[-2], weights, sems, False)

    for i, copy in enumerate(copies):

        @pl.when(step == i)
        def _(copy=copy):
            copy.wait()


def forward_kernel(n, info_ref, *refs):
    hidden_ref, pre_ref, up_ref, x, weights, x_sems, sems = refs[shares + n :]
    load(n, info_ref[0], refs[:shares], refs[shares : shares + n], x, weights, x_sems, sems)
    part = pl.program_id(0)
    inputs = x[part, : hidden_ref.shape[1]]
    gate_pre = dot(inputs, weights[0], low)
    up_pre = dot(inputs, weights[1], low)
    count = hidden_ref.shape[1]
    square = lax.broadcasted_iota(jnp.int32, (count, count), 0) == lax.broadcasted_iota(jnp.int32, (count, count), 1)
    row = x[part, pl.ds(count, 1), pl.ds(pl.multiple_of(info_ref[1] * count, 128), count)].astype(jnp.float32)
    scale = jnp.sum(jnp.where(square, row, 0.0), axis=1, keepdims=True)
    squash = 1.0 / (1.0 + jnp.exp(-gate_pre))
    active = gate_pre * squash * scale
    hidden_ref[0] = (active * up_pre).astype(jnp.bfloat16)
    slope = up_pre * squash * (1.0 + gate_pre * (1.0 - squash)) * scale
    pre_ref[0] = slope.astype(jnp.bfloat16)
    up_ref[0] = active.astype(jnp.bfloat16)


def grow_kernel(n, me_ref, slope_ref, active_ref, *refs):
    pre_ref, up_ref, u, weights, u_sems, sems = refs[shares + n :]
    load(n, me_ref[0], refs[:shares], refs[shares : shares + n], u, weights, u_sems, sems)
    d_hidden = dot(u[pl.program_id(0)], weights[...], low)
    pre_ref[0] = (d_hidden * slope_ref[0].astype(jnp.float32)).astype(jnp.bfloat16)
    up_ref[0] = (d_hidden * active_ref[0].astype(jnp.float32)).astype(jnp.bfloat16)


def on_tokens(name, kernel, prefetch, first, count, parts, blocks, outputs):
    features = parts[0].shape[1]
    n, width = len(blocks), blocks[0].shape[-1]
    each = pl.BlockSpec((1, count, width), lambda r, info: (r, 0, 0))
    return pl.pallas_call(
        functools.partial(kernel, n),
        grid_spec=pltpu.PrefetchScalarGridSpec(
            num_scalar_prefetch=1,
            grid=(shares,),
            in_specs=[each] * len(first) + [anywhere] * (shares + n),
            out_specs=[each] * outputs,
            scratch_shapes=[
                pltpu.VMEM((shares, *parts[0].shape), jnp.bfloat16),
                pltpu.VMEM((*blocks[0].shape[:-2], features, width), jnp.bfloat16),
                pltpu.SemaphoreType.DMA((shares,)),
                pltpu.SemaphoreType.DMA((n,)),
            ],
        ),
        out_shape=[jax.ShapeDtypeStruct((shares, count, width), jnp.bfloat16)] * outputs,
        compiler_params=params,
        cost_estimate=pl.CostEstimate(
            flops=2 * shares * count * n * blocks[0].size,
            bytes_accessed=2 * shares * count * features + 2 * n * blocks[0].size,
            transcendentals=0,
        ),
        name=name,
    )(prefetch, *first, *parts, *blocks)


def forward(info, count, x_parts, blocks):
    return on_tokens("forward", forward_kernel, info, [], count, x_parts, blocks, 3)


def grow(info, count, u_parts, blocks, factors):
    return on_tokens("grow", grow_kernel, info, factors, count, u_parts, blocks, 2)


def produce_kernel(keys, me_ref, ids_ref, hidden_ref, *refs):
    keep_ref, send_ref, down, sems = refs[len(keys) :]
    chunk, part = pl.program_id(0), pl.program_id(1)

    @pl.when(part == 0)
    def _():
        for start in (True, False):
            fetch(keys, refs[: len(keys)], me_ref[0], ids_ref[chunk], down.shape[0], down, sems, start)

    count, width = hidden_ref.shape[1:]
    produced = dot(hidden_ref[...].reshape(2 * count, width), down[...], high).astype(jnp.bfloat16)
    keep_ref[0, 0] = produced[:count]
    send_ref[0, 0] = produced[count:]


def produce(me, ids, chunks, hidden, keys, blocks, features):
    _, count, width = hidden.shape
    columns, size = features // chunks, ids.shape[0]
    half = pl.BlockSpec((1, 1, count, columns), lambda c, r, me, ids: (c, r, 0, 0))
    return pl.pallas_call(
        functools.partial(produce_kernel, keys),
        grid_spec=pltpu.PrefetchScalarGridSpec(
            num_scalar_prefetch=2,
            grid=(size, shares // 2),
            in_specs=[pl.BlockSpec((2, count, width), lambda c, r, me, ids: (r, 0, 0))] + [anywhere] * len(blocks),
            out_specs=[half, half],
            scratch_shapes=[pltpu.VMEM((columns, width), jnp.bfloat16), pltpu.SemaphoreType.DMA((len(keys),))],
        ),
        out_shape=[jax.ShapeDtypeStruct((size, shares // 2, count, columns), jnp.bfloat16)] * 2,
        compiler_params=params,
        cost_estimate=pl.CostEstimate(
            flops=2 * hidden.size * columns * size,
            bytes_accessed=2 * hidden.size * (size + 1),
            transcendentals=0,
        ),
        name="produce",
    )(me, ids, hidden, *blocks)


def back_kernel(n, me_ref, ids_ref, pre_ref, up_ref, *refs):
    block_refs = refs[:n]
    keep_ref, send_ref, weights, sems = refs[n:]
    chunk, part = pl.program_id(0), pl.program_id(1)
    size, span = weights.shape[0], weights.shape[2]

    for c in range(size):

        @pl.when((chunk == 0) & (part == 0))
        def _(c=c):
            fetch(range(n), block_refs, me_ref[0], ids_ref[c], span, weights.at[c], sems.at[c], True)

    for c in range(size):

        @pl.when((chunk == c) & (part == 0))
        def _(c=c):
            fetch(range(n), block_refs, me_ref[0], ids_ref[c], span, weights.at[c], sems.at[c], False)

    count, width = pre_ref.shape[1:]
    grown = dot(pre_ref[...].reshape(2 * count, width), weights[chunk, 0], high)
    grown = grown + dot(up_ref[...].reshape(2 * count, width), weights[chunk, 1], high)
    keep_ref[0, 0] = grown[:count].astype(jnp.bfloat16)
    send_ref[0, 0] = grown[count:].astype(jnp.bfloat16)


def back(me, ids, chunks, d_pre, d_up, blocks):
    _, count, width = d_pre.shape
    n, size = len(blocks), ids.shape[0]
    columns = n * blocks[0].shape[1] // chunks
    part = pl.BlockSpec((2, count, width), lambda c, r, me, ids: (r, 0, 0))
    half = pl.BlockSpec((1, 1, count, columns), lambda c, r, me, ids: (c, r, 0, 0))
    return pl.pallas_call(
        functools.partial(back_kernel, n),
        grid_spec=pltpu.PrefetchScalarGridSpec(
            num_scalar_prefetch=2,
            grid=(size, shares // 2),
            in_specs=[part, part] + [anywhere] * n,
            out_specs=[half, half],
            scratch_shapes=[
                pltpu.VMEM((size, 2, columns, width), jnp.bfloat16),
                pltpu.SemaphoreType.DMA((size, n)),
            ],
        ),
        out_shape=[jax.ShapeDtypeStruct((size, shares // 2, count, columns), jnp.bfloat16)] * 2,
        compiler_params=params,
        cost_estimate=pl.CostEstimate(
            flops=4 * size * shares * count * width * columns,
            bytes_accessed=4 * d_pre.size + 4 * size * columns * width,
            transcendentals=0,
        ),
        name="back",
    )(me, ids, d_pre, d_up, *blocks)


def pack_kernel(value_ref, scale_ref, tick_ref, out_ref):
    count, (experts, tokens) = value_ref.shape[0], scale_ref.shape
    out_ref[:count] = value_ref[...]
    if out_ref.shape[0] > count:
        out_ref[count:] = jnp.zeros((out_ref.shape[0] - count, out_ref.shape[1]), out_ref.dtype)
        for expert in range(experts):
            out_ref[pl.ds(count, 16), pl.ds(expert * tokens, tokens)] = jnp.broadcast_to(
                scale_ref[pl.ds(expert, 1), :], (16, tokens)
            ).astype(out_ref.dtype)


def pack(value, scale, tick, extra):
    return pl.pallas_call(
        pack_kernel,
        in_specs=[pl.BlockSpec(memory_space=pltpu.VMEM)] * 2 + [anywhere],
        out_specs=pl.BlockSpec(memory_space=pltpu.VMEM),
        out_shape=jax.ShapeDtypeStruct((value.shape[0] + extra, value.shape[1]), value.dtype),
        compiler_params=params,
        name="pack",
    )(value, scale, tick)


def token_scales(slot_token, slot_gate, block_expert, experts, token_count):
    block_rows = slot_token.shape[0] // block_expert.shape[0]
    scale = slot_gate.astype(jnp.float32) / gate_steps
    slot_expert = jnp.repeat(block_expert, block_rows)
    weight = jnp.where(slot_expert[None, :] == jnp.arange(experts)[:, None], scale[None, :], 0.0)
    hot = (slot_token[:, None] == jnp.arange(token_count)[None, :]).astype(jnp.bfloat16)
    return jnp.dot(weight.astype(jnp.bfloat16), hot, preferred_element_type=jnp.float32)


def shards(n, m, tokens, cotangent, w_gate, w_up, w_down, slot_token, slot_gate, block_expert):
    experts = w_gate.shape[0]
    count, features = tokens.shape
    columns = features // m
    me, z = lax.axis_index("dp"), lax.axis_index("etp")
    top, chip, here = n // 2, me // 2, me.reshape(1)
    gather_bits = [1 << i for i in range(1, n.bit_length() - 2)]
    single = len(gather_bits) == 1
    mine = (me & 1) + 2 * (me // top)
    pick = jnp.stack([mine ^ share for share in range(shares)]).astype(jnp.int32)
    clock = Clock()
    wide = functools.partial(jnp.asarray, dtype=jnp.float32)

    def shift(value, step, targets=None):
        if targets is None:
            return lax.ppermute(value, "etp", [(i, (i + step) % m) for i in range(m)])
        pairs = [
            (d * m + i, d * m + (i + step) % m)
            for d in range(n)
            for i in range(m)
            if (i + step) % m in targets(d)
        ]
        return lax.ppermute(value, ("dp", "etp"), pairs)

    have, starts, needs = {}, {}, {}
    scale = token_scales(slot_token, slot_gate, block_expert, experts, count)

    def plan(slot, until, name, source, mask):
        starts.setdefault(slot, []).append((name, source, mask))
        needs.setdefault(until, []).append(name)

    plan(0, 1, ("rows", 1), ("rows piece", 1), 1)
    plan(0, 2, ("rows", top), ("rows piece", 2), top)
    plan(1, 3, ("rows", top + 1), ("rows piece", 3), top + 1)
    plan(2, 3, ("turned", top), ("turned piece", 2), top)
    plan(3, 6, "x near", "x", 1)
    plan(3, 5, "x far", "x", top)
    plan(3, 5, ("turned", 1), ("turned piece", 1), 1)
    plan(4, 8, ("turned", top + 1), ("turned piece", 3), top + 1)
    plan(5, 6, "x far near", "x far", 1)
    plan(6, 8, "u far", "u", top)
    plan(4, 8, "u near", "u", 1)
    plan(8, 9, "u far near", "u far", 1)
    slots = [(0, 2), (1, 3), (2, 4), (3, 5), (4, 6), (5, 7), (7, 9), (8, 9)]
    moves = 0
    for kind in ("rows", "turned"):
        held = [0, 1, top, top + 1]
        for bit in gather_bits:
            for key in list(held):
                begin, until = slots[moves] if single else (moves + 3, moves + 5)
                plan(begin, until, (kind, key ^ bit), (kind, key), bit)
                held.append(key ^ bit)
                moves += 1

    def tick(at, extra=()):
        begin = starts.get(at, [])
        names = list(dict.fromkeys(source for _, source, _ in begin))
        wait = [have[name] for name in needs.get(at, [])]
        have.update(zip(names, clock.tick([have[name] for name in names], [*wait, *extra])))
        for name, source, mask in begin:
            have[name] = swap(have[source], mask, n)

    pieces = cast_rows(pick, w_gate, w_up)
    have["rows", 0] = pieces[0]
    have.update({("rows piece", share): pieces[share] for share in range(1, shares)})
    tick(0)
    pieces = cast_turned(pick, w_down, clock.token)
    have["turned", 0] = pieces[0]
    have.update({("turned piece", share): pieces[share] for share in range(1, shares)})
    tick(1)
    have["x"] = pack(tokens, scale, clock.token, 16)
    tick(2)
    have["u"] = pack(cotangent, scale, clock.token, 0)
    last = max(needs)
    halves = n == 2 * m and single
    for at in range(3, 7 if halves else last + 1):
        tick(at)

    blocks = [have["rows", key] for key in range(n)]
    info = jnp.stack([me, mine // (shares // experts)]).astype(jnp.int32)
    hidden, *factors = forward(info, count, [have[k] for k in ("x", "x near", "x far", "x far near")], blocks)

    def run(keys, ids, hidden):
        return produce(here, ids, m, hidden, keys, [have["turned", key] for key in keys], features)

    def add(keep, near):
        return (wide(keep[:, 1]) + wide(near[:, 1])).astype(jnp.bfloat16), wide(keep[:, 0]) + wide(near[:, 0])

    def choose(target, keys, values):
        if keys is None:
            return lax.dynamic_index_in_dim(jnp.stack(list(values)), target, 0, False)
        return jnp.where(target == chip ^ (keys[0] // 2), values[0], values[1])

    order = [m // 2] + [step for step in range(1, m) if step != m // 2] + [0]

    def outward(total, keys):
        own = choose(z, keys, total)
        if keys is not None:
            there = (z == chip ^ (keys[0] // 2)) | (z == chip ^ (keys[1] // 2))
            own = jnp.where(there, own, 0.0)
        total = [part.astype(jnp.bfloat16) for part in total]
        return own, [choose(lax.rem(z + step, m), keys, total) for step in order[:-1]]

    def pass_on(values, keys):
        targets = None if keys is None else lambda d: [(d ^ key) // 2 for key in keys]
        return [shift(value, step, targets) for value, step in zip(values, order)]

    gained, u_names = [], ("u", "u near", "u far", "u far near")
    downs = lambda: [have["turned", key] for key in range(n)]
    if halves:
        bit = gather_bits[0]
        tick(7, [hidden])
        keep_a, send_a = run([0, 1, top, top + 1], jnp.stack([chip, chip ^ (top // 2)]), hidden)
        tick(8, [send_a])
        (send_a,) = clock.tick([send_a])
        near = swap(send_a, 1, n)
        keep_b, send_b = run([bit, bit + 1], (chip ^ (bit // 2)).reshape(1), hidden)
        (send_b,) = clock.tick([send_b], [near, have["turned", top ^ bit]])
        other, own_a = add(keep_a, near)
        near = swap(send_b, 1, n)
        (other,) = clock.tick([other], [near])
        far_a = swap(other, top, n)
        other, own_b = add(keep_b, near)
        (other,) = clock.tick([other], [have["turned", top ^ bit ^ 1]])
        far_b = swap(other, top, n)
        clock.tick([], [far_a, far_b])
        own, values = outward([own_a[0] + wide(far_a[1]), own_a[1] + wide(far_a[0])], (0, top))
        values = clock.tick(values)
        gained.append(own)
        early = pass_on(values, (0, top))
        gained += [wide(value) for value in early]
        tick(9)
        (hidden,) = clock.tick([hidden])
        ids, keys = (chip ^ ((bit ^ top) // 2)).reshape(1), [bit + top, bit + top + 1]
    else:
        ids, keys, early = jnp.arange(m, dtype=jnp.int32), list(range(n)), []
    keep, send = run(keys, ids, hidden)
    u_parts = [have[name] for name in u_names]
    send, u_parts[0] = clock.tick([send, u_parts[0]])
    near = swap(send, 1, n)
    d_pre, d_up = grow(info, count, u_parts, downs(), factors)
    (d_pre,) = clock.tick([d_pre], [near])
    other, own = add(keep, near)
    (other,) = clock.tick([other])
    got = swap(other, top, n)
    steps = jnp.array([order[: m // 2], order[m // 2 :]], jnp.int32)
    keep_0, send_0 = back(here, lax.rem(z + steps[0], m), m, d_pre, d_up, blocks)
    send_0, d_pre = clock.tick([send_0, d_pre], early)
    near_0 = swap(send_0, 1, n)
    keep_1, send_1 = back(here, lax.rem(z + steps[1], m), m, d_pre, d_up, blocks)
    (send_1,) = clock.tick([send_1], [near_0, got])
    near_1 = swap(send_1, 1, n)
    other, own_0 = add(keep_0, near_0)
    (other,) = clock.tick([other])
    got_0 = swap(other, top, n)
    if halves:
        total = [own_b[0] + wide(got[0]), own[0] + wide(far_b[0])]
        keys = (bit, bit ^ top)
    else:
        total, keys = own + wide(got), None
    own, values = outward(total, keys)
    values = clock.tick(values, [near_1])
    gained.append(own)
    gained += [wide(value) for value in pass_on(values, keys)]
    other, own_1 = add(keep_1, near_1)
    (other,) = clock.tick([other])
    got_1 = swap(other, top, n)
    clock.tick([], [got_0])
    owns, gots = [own_0, own_1], [got_0, got_1]
    combined = sum(gained)
    grad = 0.0
    for i, step in enumerate(order):
        half, at = divmod(i, m // 2)
        value = owns[half][at] + wide(gots[half][at])
        if step:
            (value,) = clock.tick([value.astype(jnp.bfloat16)])
            value = wide(shift(value, step))
        grad = grad + value
    return combined.astype(jnp.bfloat16), grad.astype(jnp.bfloat16)


def solution(mesh):
    in_specs = (
        P("dp", None),
        P("dp", None),
        P(None, "dp", "etp"),
        P(None, "dp", "etp"),
        P(None, "etp", "dp"),
        P("dp"),
        P("dp"),
        P("dp"),
    )
    out_specs = (P("dp", "etp"), P("dp", "etp"))
    body = functools.partial(shards, mesh.shape["dp"], mesh.shape["etp"])
    return jax.shard_map(body, mesh=mesh, in_specs=in_specs, out_specs=out_specs, check_vma=False)
```

```python
import functools

import jax
import jax.numpy as jnp
from jax import lax
from jax.experimental import pallas as pl
from jax.experimental.pallas import tpu as pltpu
from jax.sharding import PartitionSpec as P

gate_steps = 16.0
vmem_limit = 48 * 1024 * 1024
shares = 4
slot_us = 5.0
flop_rate = 1_150_000_000
low, high = (((1,), (0,)), ((), ())), (((1,), (1,)), ((), ()))
dot = functools.partial(lax.dot_general, preferred_element_type=jnp.float32)
params = pltpu.CompilerParams(vmem_limit_bytes=vmem_limit)
anywhere = pl.BlockSpec(memory_space=pl.ANY)


def shape_of(value):
    return jax.ShapeDtypeStruct(value.shape, value.dtype)


class Clock:
    def __init__(self):
        self.token = blank((16, 128))

    def tick(self, release, wait=()):
        held = [self.token, *release]
        known = {id(value) for value in held}
        wait = [value for value in wait if id(value) not in known]
        self.token, *out = pl.pallas_call(
            lambda *refs: None,
            in_specs=[anywhere] * (len(held) + len(wait)),
            out_specs=[anywhere] * len(held),
            out_shape=[shape_of(value) for value in held],
            input_output_aliases={i: i for i in range(len(held))},
            cost_estimate=pl.CostEstimate(flops=int(slot_us * flop_rate), bytes_accessed=0, transcendentals=0),
            name="tick",
        )(*held, *wait)
        return out


def blank(shape):
    return pl.pallas_call(
        lambda *refs: None,
        out_specs=anywhere,
        out_shape=jax.ShapeDtypeStruct(shape, jnp.bfloat16),
        name="blank",
    )()


def swap(value, mask, size):
    return lax.ppermute(value, "dp", [(i, i ^ mask) for i in range(size)])


def steps_of(rows):
    return max(step for step in (1, 2, 4) if rows % (16 * step) == 0)


def cast_rows_kernel(pick_ref, gate_ref, up_ref, *out_refs):
    parts = shares // gate_ref.shape[0]
    width = out_refs[0].shape[-1]
    for share, out_ref in enumerate(out_refs):
        expert = pick_ref[share] // parts
        lanes = pl.ds(pl.multiple_of(pick_ref[share] % parts * width, 128), width)
        out_ref[0] = gate_ref[expert, :, lanes].astype(jnp.bfloat16)
        out_ref[1] = up_ref[expert, :, lanes].astype(jnp.bfloat16)


def cast_rows(pick, w_gate, w_up):
    experts, rows, hidden = w_gate.shape
    width = experts * hidden // shares
    steps = steps_of(rows)
    block = pl.BlockSpec((experts, rows // steps, hidden), lambda i, pick: (0, i, 0))
    return pl.pallas_call(
        cast_rows_kernel,
        grid_spec=pltpu.PrefetchScalarGridSpec(
            num_scalar_prefetch=1,
            grid=(steps,),
            in_specs=[block, block],
            out_specs=[pl.BlockSpec((2, rows // steps, width), lambda i, pick: (0, i, 0))] * shares,
        ),
        out_shape=[pltpu.HBM((2, rows, width), jnp.bfloat16)] * shares,
        compiler_params=params,
        name="cast_rows",
    )(pick, w_gate, w_up)


def cast_turned_kernel(pick_ref, down_ref, *refs):
    out_refs = refs[-shares:]
    parts = shares // down_ref.shape[0]
    width = out_refs[0].shape[-1]
    for share, out_ref in enumerate(out_refs):
        expert = pick_ref[share] // parts
        rows = pl.ds(pl.multiple_of(pick_ref[share] % parts * width, 128), width)
        out_ref[...] = down_ref[expert, rows, :].T.astype(jnp.bfloat16)


def cast_turned(pick, w_down, *earlier):
    experts, hidden, features = w_down.shape
    width = experts * hidden // shares
    tile = 128 if features % 128 == 0 else features
    return pl.pallas_call(
        cast_turned_kernel,
        grid_spec=pltpu.PrefetchScalarGridSpec(
            num_scalar_prefetch=1,
            grid=(features // tile,),
            in_specs=[pl.BlockSpec((experts, hidden, tile), lambda i, pick: (0, 0, i))]
            + [anywhere] * len(earlier),
            out_specs=[pl.BlockSpec((tile, width), lambda i, pick: (i, 0))] * shares,
        ),
        out_shape=[pltpu.HBM((features, width), jnp.bfloat16)] * shares,
        compiler_params=params,
        name="cast_turned",
    )(pick, w_down, *earlier)


def fetch(keys, refs, me, chunk, span, target, sems, start):
    rows = refs[0].shape[-2]
    per = span // rows
    for i, (key, ref) in enumerate(zip(keys, refs)):
        block = me ^ key

        @pl.when(block // per == chunk)
        def _(ref=ref, i=i, block=block):
            place = pl.ds(pl.multiple_of(block % per * rows, 16), rows)
            view = target.at[place] if len(target.shape) == 2 else target.at[:, place]
            copy = pltpu.make_async_copy(ref, view, sems.at[i])
            if start:
                copy.start()
            else:
                copy.wait()


def load(n, me, parts, blocks, x, weights, x_sems, sems):
    step = pl.program_id(0)
    copies = [pltpu.make_async_copy(part, x.at[i], x_sems.at[i]) for i, part in enumerate(parts)]

    @pl.when(step == 0)
    def _():
        fetch(range(n), blocks, me, 0, weights.shape[-2], weights, sems, True)
        for copy in copies:
            copy.start()
        fetch(range(n), blocks, me, 0, weights.shape[-2], weights, sems, False)

    for i, copy in enumerate(copies):

        @pl.when(step == i)
        def _(copy=copy):
            copy.wait()


def forward_kernel(n, info_ref, *refs):
    hidden_ref, pre_ref, up_ref, x, weights, x_sems, sems = refs[shares + n :]
    load(n, info_ref[0], refs[:shares], refs[shares : shares + n], x, weights, x_sems, sems)
    part = pl.program_id(0)
    inputs = x[part, : hidden_ref.shape[1]]
    gate_pre = dot(inputs, weights[0], low)
    up_pre = dot(inputs, weights[1], low)
    count = hidden_ref.shape[1]
    square = lax.broadcasted_iota(jnp.int32, (count, count), 0) == lax.broadcasted_iota(jnp.int32, (count, count), 1)
    row = x[part, pl.ds(count, 1), pl.ds(pl.multiple_of(info_ref[1] * count, 128), count)].astype(jnp.float32)
    scale = jnp.sum(jnp.where(square, row, 0.0), axis=1, keepdims=True)
    squash = 1.0 / (1.0 + jnp.exp(-gate_pre))
    active = gate_pre * squash * scale
    hidden_ref[0] = (active * up_pre).astype(jnp.bfloat16)
    slope = up_pre * squash * (1.0 + gate_pre * (1.0 - squash)) * scale
    pre_ref[0] = slope.astype(jnp.bfloat16)
    up_ref[0] = active.astype(jnp.bfloat16)


def grow_kernel(n, me_ref, slope_ref, active_ref, *refs):
    pre_ref, up_ref, u, weights, u_sems, sems = refs[shares + n :]
    load(n, me_ref[0], refs[:shares], refs[shares : shares + n], u, weights, u_sems, sems)
    d_hidden = dot(u[pl.program_id(0)], weights[...], low)
    pre_ref[0] = (d_hidden * slope_ref[0].astype(jnp.float32)).astype(jnp.bfloat16)
    up_ref[0] = (d_hidden * active_ref[0].astype(jnp.float32)).astype(jnp.bfloat16)


def on_tokens(name, kernel, prefetch, first, count, parts, blocks, outputs):
    features = parts[0].shape[1]
    n, width = len(blocks), blocks[0].shape[-1]
    each = pl.BlockSpec((1, count, width), lambda r, info: (r, 0, 0))
    return pl.pallas_call(
        functools.partial(kernel, n),
        grid_spec=pltpu.PrefetchScalarGridSpec(
            num_scalar_prefetch=1,
            grid=(shares,),
            in_specs=[each] * len(first) + [anywhere] * (shares + n),
            out_specs=[each] * outputs,
            scratch_shapes=[
                pltpu.VMEM((shares, *parts[0].shape), jnp.bfloat16),
                pltpu.VMEM((*blocks[0].shape[:-2], features, width), jnp.bfloat16),
                pltpu.SemaphoreType.DMA((shares,)),
                pltpu.SemaphoreType.DMA((n,)),
            ],
        ),
        out_shape=[jax.ShapeDtypeStruct((shares, count, width), jnp.bfloat16)] * outputs,
        compiler_params=params,
        cost_estimate=pl.CostEstimate(
            flops=2 * shares * count * n * blocks[0].size,
            bytes_accessed=2 * shares * count * features + 2 * n * blocks[0].size,
            transcendentals=0,
        ),
        name=name,
    )(prefetch, *first, *parts, *blocks)


def forward(info, count, x_parts, blocks):
    return on_tokens("forward", forward_kernel, info, [], count, x_parts, blocks, 3)


def grow(info, count, u_parts, blocks, factors):
    return on_tokens("grow", grow_kernel, info, factors, count, u_parts, blocks, 2)


def produce_kernel(keys, me_ref, ids_ref, hidden_ref, *refs):
    keep_ref, send_ref, down, sems = refs[len(keys) :]
    chunk, part = pl.program_id(0), pl.program_id(1)

    @pl.when(part == 0)
    def _():
        for start in (True, False):
            fetch(keys, refs[: len(keys)], me_ref[0], ids_ref[chunk], down.shape[0], down, sems, start)

    count, width = hidden_ref.shape[1:]
    produced = dot(hidden_ref[...].reshape(2 * count, width), down[...], high).astype(jnp.bfloat16)
    keep_ref[0, 0] = produced[:count]
    send_ref[0, 0] = produced[count:]


def produce(me, ids, chunks, hidden, keys, blocks, features):
    _, count, width = hidden.shape
    columns, size = features // chunks, ids.shape[0]
    half = pl.BlockSpec((1, 1, count, columns), lambda c, r, me, ids: (c, r, 0, 0))
    return pl.pallas_call(
        functools.partial(produce_kernel, keys),
        grid_spec=pltpu.PrefetchScalarGridSpec(
            num_scalar_prefetch=2,
            grid=(size, shares // 2),
            in_specs=[pl.BlockSpec((2, count, width), lambda c, r, me, ids: (r, 0, 0))] + [anywhere] * len(blocks),
            out_specs=[half, half],
            scratch_shapes=[pltpu.VMEM((columns, width), jnp.bfloat16), pltpu.SemaphoreType.DMA((len(keys),))],
        ),
        out_shape=[pltpu.HBM((size, shares // 2, count, columns), jnp.bfloat16)] * 2,
        compiler_params=params,
        cost_estimate=pl.CostEstimate(
            flops=2 * hidden.size * columns * size,
            bytes_accessed=2 * hidden.size * (size + 1),
            transcendentals=0,
        ),
        name="produce",
    )(me, ids, hidden, *blocks)


def back_kernel(n, me_ref, ids_ref, pre_ref, up_ref, *refs):
    block_refs = refs[:n]
    keep_ref, send_ref, weights, sems = refs[n:]
    chunk, part = pl.program_id(0), pl.program_id(1)
    size, span = weights.shape[0], weights.shape[2]

    for c in range(size):

        @pl.when((chunk == 0) & (part == 0))
        def _(c=c):
            fetch(range(n), block_refs, me_ref[0], ids_ref[c], span, weights.at[c], sems.at[c], True)

    for c in range(size):

        @pl.when((chunk == c) & (part == 0))
        def _(c=c):
            fetch(range(n), block_refs, me_ref[0], ids_ref[c], span, weights.at[c], sems.at[c], False)

    count, width = pre_ref.shape[1:]
    grown = dot(pre_ref[...].reshape(2 * count, width), weights[chunk, 0], high)
    grown = grown + dot(up_ref[...].reshape(2 * count, width), weights[chunk, 1], high)
    keep_ref[0, 0] = grown[:count].astype(jnp.bfloat16)
    send_ref[0, 0] = grown[count:].astype(jnp.bfloat16)


def back(me, ids, chunks, d_pre, d_up, blocks):
    _, count, width = d_pre.shape
    n, size = len(blocks), ids.shape[0]
    columns = n * blocks[0].shape[1] // chunks
    part = pl.BlockSpec((2, count, width), lambda c, r, me, ids: (r, 0, 0))
    half = pl.BlockSpec((1, 1, count, columns), lambda c, r, me, ids: (c, r, 0, 0))
    return pl.pallas_call(
        functools.partial(back_kernel, n),
        grid_spec=pltpu.PrefetchScalarGridSpec(
            num_scalar_prefetch=2,
            grid=(size, shares // 2),
            in_specs=[part, part] + [anywhere] * n,
            out_specs=[half, half],
            scratch_shapes=[
                pltpu.VMEM((size, 2, columns, width), jnp.bfloat16),
                pltpu.SemaphoreType.DMA((size, n)),
            ],
        ),
        out_shape=[pltpu.HBM((size, shares // 2, count, columns), jnp.bfloat16)] * 2,
        compiler_params=params,
        cost_estimate=pl.CostEstimate(
            flops=4 * size * shares * count * width * columns,
            bytes_accessed=4 * d_pre.size + 4 * size * columns * width,
            transcendentals=0,
        ),
        name="back",
    )(me, ids, d_pre, d_up, *blocks)


def pack_kernel(value_ref, scale_ref, tick_ref, out_ref):
    count, (experts, tokens) = value_ref.shape[0], scale_ref.shape
    out_ref[:count] = value_ref[...]
    if out_ref.shape[0] > count:
        out_ref[count:] = jnp.zeros((out_ref.shape[0] - count, out_ref.shape[1]), out_ref.dtype)
        for expert in range(experts):
            out_ref[pl.ds(count, 16), pl.ds(expert * tokens, tokens)] = jnp.broadcast_to(
                scale_ref[pl.ds(expert, 1), :], (16, tokens)
            ).astype(out_ref.dtype)


def pack(value, scale, tick, extra):
    return pl.pallas_call(
        pack_kernel,
        in_specs=[pl.BlockSpec(memory_space=pltpu.VMEM)] * 2 + [anywhere],
        out_specs=pl.BlockSpec(memory_space=pltpu.VMEM),
        out_shape=jax.ShapeDtypeStruct((value.shape[0] + extra, value.shape[1]), value.dtype),
        compiler_params=params,
        name="pack",
    )(value, scale, tick)


def token_scales(slot_token, slot_gate, block_expert, experts, token_count):
    block_rows = slot_token.shape[0] // block_expert.shape[0]
    scale = slot_gate.astype(jnp.float32) / gate_steps
    slot_expert = jnp.repeat(block_expert, block_rows)
    weight = jnp.where(slot_expert[None, :] == jnp.arange(experts)[:, None], scale[None, :], 0.0)
    hot = (slot_token[:, None] == jnp.arange(token_count)[None, :]).astype(jnp.bfloat16)
    return jnp.dot(weight.astype(jnp.bfloat16), hot, preferred_element_type=jnp.float32)


def shards(n, m, tokens, cotangent, w_gate, w_up, w_down, slot_token, slot_gate, block_expert):
    experts = w_gate.shape[0]
    count, features = tokens.shape
    columns = features // m
    me, z = lax.axis_index("dp"), lax.axis_index("etp")
    top, chip, here = n // 2, me // 2, me.reshape(1)
    gather_bits = [1 << i for i in range(1, n.bit_length() - 2)]
    single = len(gather_bits) == 1
    mine = (me & 1) + 2 * (me // top)
    pick = jnp.stack([mine ^ share for share in range(shares)]).astype(jnp.int32)
    clock = Clock()
    wide = functools.partial(jnp.asarray, dtype=jnp.float32)

    def shift(value, step):
        return lax.ppermute(value, "etp", [(i, (i + step) % m) for i in range(m)])

    have, starts, needs = {}, {}, {}
    scale = token_scales(slot_token, slot_gate, block_expert, experts, count)

    def plan(slot, until, name, source, mask):
        starts.setdefault(slot, []).append((name, source, mask))
        needs.setdefault(until, []).append(name)

    plan(0, 1, ("rows", 1), ("rows piece", 1), 1)
    plan(0, 2, ("rows", top), ("rows piece", 2), top)
    plan(1, 3, ("rows", top + 1), ("rows piece", 3), top + 1)
    plan(1, 2, ("turned", 1), ("turned piece", 1), 1)
    plan(2, 3, ("turned", top), ("turned piece", 2), top)
    plan(3, 5, "x far", "x", top)
    plan(3, 5, "x near", "x", 1)
    plan(3, 5, ("turned", top + 1), ("turned piece", 3), top + 1)
    plan(5, 6, "x far near", "x far", 1)
    plan(6, 8, "u far", "u", top)
    plan(6, 8, "u near", "u", 1)
    plan(8, 9, "u far near", "u far", 1)
    slots = [(0, 2), (1, 3), (2, 4), (3, 5), (4, 5), (5, 7), (5, 7), (6, 8)]
    moves = 0
    for kind in ("rows", "turned"):
        held = [0, 1, top, top + 1]
        for bit in gather_bits:
            for key in list(held):
                begin, until = slots[moves] if single else (moves + 3, moves + 5)
                plan(begin, until, (kind, key ^ bit), (kind, key), bit)
                held.append(key ^ bit)
                moves += 1

    def tick(at, extra=()):
        begin = starts.get(at, [])
        names = list(dict.fromkeys(source for _, source, _ in begin))
        wait = [have[name] for name in needs.get(at, [])]
        have.update(zip(names, clock.tick([have[name] for name in names], [*wait, *extra])))
        for name, source, mask in begin:
            have[name] = swap(have[source], mask, n)

    pieces = cast_rows(pick, w_gate, w_up)
    have["rows", 0] = pieces[0]
    have.update({("rows piece", share): pieces[share] for share in range(1, shares)})
    tick(0)
    pieces = cast_turned(pick, w_down, clock.token)
    have["turned", 0] = pieces[0]
    have.update({("turned piece", share): pieces[share] for share in range(1, shares)})
    tick(1)
    have["x"] = pack(tokens, scale, clock.token, 16)
    tick(2)
    have["u"] = pack(cotangent, scale, clock.token, 0)
    last = max(needs)
    halves = n == 2 * m and single
    for at in range(3, 7 if halves else last + 1):
        tick(at)

    def hold(values, *wait):
        (first,) = clock.tick(values[:1], wait)
        return [first, *values[1:]]

    blocks = hold([have["rows", key] for key in range(n)])
    info = jnp.stack([me, mine // (shares // experts)]).astype(jnp.int32)
    hidden, *factors = forward(info, count, [have[k] for k in ("x", "x near", "x far", "x far near")], blocks)

    def run(keys, ids, hidden):
        return produce(here, ids, m, hidden, keys, [have["turned", key] for key in keys], features)

    def add(keep, near):
        return (wide(keep[:, 1]) + wide(near[:, 1])).astype(jnp.bfloat16), wide(keep[:, 0]) + wide(near[:, 0])

    order = [m // 2] + [step for step in range(1, m) if step != m // 2] + [0]

    if halves:
        bit = gather_bits[0]
        first, second = [0, top], [bit, bit ^ top]
        tick(7, [hidden])
        keep_a, send_a = run([0, 1, top, top + 1], jnp.stack([chip ^ (key // 2) for key in first]), hidden)
        (send_a,) = clock.tick([send_a], [have["u far"], have["turned", top + 1 + bit]])
        near_a = swap(send_a, 1, n)
        tick(8)
        tick(9)
        keys = [bit, bit + 1, bit + top, bit + top + 1]
        have["turned", bit] = hold([have["turned", bit]], near_a)[0]
        keep, send = run(keys, jnp.stack([chip ^ (key // 2) for key in second]), hidden)
        (send,) = clock.tick([send])
        near = swap(send, 1, n)
        other, own_a = add(keep_a, near_a)
        (other,) = clock.tick([other])
        far_a = swap(other, top, n)
    else:
        keep, send = run(list(range(n)), jnp.arange(m, dtype=jnp.int32), hidden)
        near = swap(send, 1, n)
    clock.tick([], [near])
    other, own = add(keep, near)
    (other,) = clock.tick([other])
    got = swap(other, top, n)
    u_parts = hold([have[name] for name in ("u", "u near", "u far", "u far near")])
    d_pre, d_up = grow(info, count, u_parts, [have["turned", key] for key in range(n)], factors)
    steps = jnp.array([order[: m // 2], order[m // 2 :]], jnp.int32)
    blocks = hold(blocks, d_pre)
    keep_0, send_0 = back(here, lax.rem(z + steps[0], m), m, d_pre, d_up, blocks)
    (send_0,) = clock.tick([send_0], [far_a, got] if halves else [got])
    near_0 = swap(send_0, 1, n)
    if halves:
        sums = [own_a[0] + wide(far_a[1]), own_a[1] + wide(far_a[0]), own[0] + wide(got[1]), own[1] + wide(got[0])]
        where = [chip ^ (key // 2) for key in first + second]
    else:
        sums = list(own + wide(got))
        where = list(range(m))

    def chunk_of(target, values):
        chosen = values[-1]
        for value, place in zip(values[:-1], where):
            chosen = jnp.where(target == place, value, chosen)
        return chosen

    combined = chunk_of(z, sums)
    low_sums = [value.astype(jnp.bfloat16) for value in sums]
    values = clock.tick([chunk_of(lax.rem(z + step, m), low_sums) for step in order[:-1]])
    late = [shift(value, step) for value, step in zip(values, order)]
    clock.tick([], [near_0])
    other, own_0 = add(keep_0, near_0)
    (other,) = clock.tick([other])
    got_0 = swap(other, top, n)
    blocks = hold(blocks)
    keep_1, send_1 = back(here, lax.rem(z + steps[1], m), m, d_pre, d_up, blocks)
    (send_1,) = clock.tick([send_1], [got_0, *late[1:]])
    near_1 = swap(send_1, 1, n)
    clock.tick([], [near_1])
    other, own_1 = add(keep_1, near_1)
    (other,) = clock.tick([other])
    got_1 = swap(other, top, n)
    for value in late:
        combined = combined + wide(value)
    owns, gots = [own_0, own_1], [got_0, got_1]
    grad = 0.0
    for i, step in enumerate(order):
        half, at = divmod(i, m // 2)
        value = owns[half][at] + wide(gots[half][at])
        if step:
            (value,) = clock.tick([value.astype(jnp.bfloat16)], late[:1] if i == 0 else [])
            value = wide(shift(value, step))
        grad = grad + value
    return combined.astype(jnp.bfloat16), grad.astype(jnp.bfloat16)


def solution(mesh):
    in_specs = (
        P("dp", None),
        P("dp", None),
        P(None, "dp", "etp"),
        P(None, "dp", "etp"),
        P(None, "etp", "dp"),
        P("dp"),
        P("dp"),
        P("dp"),
    )
    out_specs = (P("dp", "etp"), P("dp", "etp"))
    body = functools.partial(shards, mesh.shape["dp"], mesh.shape["etp"])
    return jax.shard_map(body, mesh=mesh, in_specs=in_specs, out_specs=out_specs, check_vma=False)
```

```python
import functools

import jax
import jax.numpy as jnp
from jax import lax
from jax.experimental import pallas as pl
from jax.experimental.pallas import tpu as pltpu
from jax.sharding import PartitionSpec as P

gate_steps = 16.0
vmem_limit = 48 * 1024 * 1024
shares = 4
slot_us = 5.0
flop_rate = 1_150_000_000
low, high = (((1,), (0,)), ((), ())), (((1,), (1,)), ((), ()))
dot = functools.partial(lax.dot_general, preferred_element_type=jnp.float32)
params = pltpu.CompilerParams(vmem_limit_bytes=vmem_limit)
anywhere = pl.BlockSpec(memory_space=pl.ANY)


def shape_of(value):
    return jax.ShapeDtypeStruct(value.shape, value.dtype)


class Clock:
    def __init__(self):
        self.token = blank((16, 128))

    def tick(self, release, wait=()):
        held = [self.token, *release]
        known = {id(value) for value in held}
        wait = [value for value in wait if id(value) not in known]
        self.token, *out = pl.pallas_call(
            lambda *refs: None,
            in_specs=[anywhere] * (len(held) + len(wait)),
            out_specs=[anywhere] * len(held),
            out_shape=[shape_of(value) for value in held],
            input_output_aliases={i: i for i in range(len(held))},
            cost_estimate=pl.CostEstimate(flops=int(slot_us * flop_rate), bytes_accessed=0, transcendentals=0),
            name="tick",
        )(*held, *wait)
        return out


def far_off(values):
    return [pltpu.with_memory_space_constraint(value, pltpu.HBM) for value in values]


def blank(shape):
    return pl.pallas_call(
        lambda *refs: None,
        out_specs=anywhere,
        out_shape=jax.ShapeDtypeStruct(shape, jnp.bfloat16),
        name="blank",
    )()


def swap(value, mask, size):
    return lax.ppermute(value, "dp", [(i, i ^ mask) for i in range(size)])


def steps_of(rows):
    return max(step for step in (1, 2, 4) if rows % (16 * step) == 0)


def cast_rows_kernel(pick_ref, gate_ref, up_ref, *out_refs):
    parts = shares // gate_ref.shape[0]
    width = out_refs[0].shape[-1]
    for share, out_ref in enumerate(out_refs):
        expert = pick_ref[share] // parts
        lanes = pl.ds(pl.multiple_of(pick_ref[share] % parts * width, 128), width)
        out_ref[0] = gate_ref[expert, :, lanes].astype(jnp.bfloat16)
        out_ref[1] = up_ref[expert, :, lanes].astype(jnp.bfloat16)


def cast_rows(pick, w_gate, w_up):
    experts, rows, hidden = w_gate.shape
    width = experts * hidden // shares
    steps = steps_of(rows)
    block = pl.BlockSpec((experts, rows // steps, hidden), lambda i, pick: (0, i, 0))
    return pl.pallas_call(
        cast_rows_kernel,
        grid_spec=pltpu.PrefetchScalarGridSpec(
            num_scalar_prefetch=1,
            grid=(steps,),
            in_specs=[block, block],
            out_specs=[pl.BlockSpec((2, rows // steps, width), lambda i, pick: (0, i, 0))] * shares,
        ),
        out_shape=[pltpu.HBM((2, rows, width), jnp.bfloat16)] * shares,
        compiler_params=params,
        name="cast_rows",
    )(pick, w_gate, w_up)


def cast_turned_kernel(pick_ref, down_ref, *refs):
    out_refs = refs[-shares:]
    parts = shares // down_ref.shape[0]
    width = out_refs[0].shape[-1]
    for share, out_ref in enumerate(out_refs):
        expert = pick_ref[share] // parts
        rows = pl.ds(pl.multiple_of(pick_ref[share] % parts * width, 128), width)
        out_ref[...] = down_ref[expert, rows, :].T.astype(jnp.bfloat16)


def cast_turned(pick, w_down, *earlier):
    experts, hidden, features = w_down.shape
    width = experts * hidden // shares
    tile = 128 if features % 128 == 0 else features
    return pl.pallas_call(
        cast_turned_kernel,
        grid_spec=pltpu.PrefetchScalarGridSpec(
            num_scalar_prefetch=1,
            grid=(features // tile,),
            in_specs=[pl.BlockSpec((experts, hidden, tile), lambda i, pick: (0, 0, i))]
            + [anywhere] * len(earlier),
            out_specs=[pl.BlockSpec((tile, width), lambda i, pick: (i, 0))] * shares,
        ),
        out_shape=[pltpu.HBM((features, width), jnp.bfloat16)] * shares,
        compiler_params=params,
        name="cast_turned",
    )(pick, w_down, *earlier)


def fetch(keys, refs, me, chunk, span, target, sems, start):
    rows = refs[0].shape[-2]
    per = span // rows
    for i, (key, ref) in enumerate(zip(keys, refs)):
        block = me ^ key

        @pl.when(block // per == chunk)
        def _(ref=ref, i=i, block=block):
            place = pl.ds(pl.multiple_of(block % per * rows, 16), rows)
            view = target.at[place] if len(target.shape) == 2 else target.at[:, place]
            copy = pltpu.make_async_copy(ref, view, sems.at[i])
            if start:
                copy.start()
            else:
                copy.wait()


def load(n, me, parts, blocks, x, weights, x_sems, sems):
    step = pl.program_id(0)
    copies = [pltpu.make_async_copy(part, x.at[i], x_sems.at[i]) for i, part in enumerate(parts)]

    @pl.when(step == 0)
    def _():
        fetch(range(n), blocks, me, 0, weights.shape[-2], weights, sems, True)
        for copy in copies:
            copy.start()
        fetch(range(n), blocks, me, 0, weights.shape[-2], weights, sems, False)

    for i, copy in enumerate(copies):

        @pl.when(step == i)
        def _(copy=copy):
            copy.wait()


def forward_kernel(n, info_ref, *refs):
    hidden_ref, pre_ref, up_ref, x, weights, x_sems, sems = refs[shares + n :]
    load(n, info_ref[0], refs[:shares], refs[shares : shares + n], x, weights, x_sems, sems)
    part = pl.program_id(0)
    inputs = x[part, : hidden_ref.shape[1]]
    gate_pre = dot(inputs, weights[0], low)
    up_pre = dot(inputs, weights[1], low)
    count = hidden_ref.shape[1]
    square = lax.broadcasted_iota(jnp.int32, (count, count), 0) == lax.broadcasted_iota(jnp.int32, (count, count), 1)
    row = x[part, pl.ds(count, 1), pl.ds(pl.multiple_of(info_ref[1] * count, 128), count)].astype(jnp.float32)
    scale = jnp.sum(jnp.where(square, row, 0.0), axis=1, keepdims=True)
    squash = 1.0 / (1.0 + jnp.exp(-gate_pre))
    active = gate_pre * squash * scale
    hidden_ref[0] = (active * up_pre).astype(jnp.bfloat16)
    slope = up_pre * squash * (1.0 + gate_pre * (1.0 - squash)) * scale
    pre_ref[0] = slope.astype(jnp.bfloat16)
    up_ref[0] = active.astype(jnp.bfloat16)


def grow_kernel(n, me_ref, slope_ref, active_ref, *refs):
    pre_ref, up_ref, u, weights, u_sems, sems = refs[shares + n :]
    load(n, me_ref[0], refs[:shares], refs[shares : shares + n], u, weights, u_sems, sems)
    d_hidden = dot(u[pl.program_id(0)], weights[...], low)
    pre_ref[0] = (d_hidden * slope_ref[0].astype(jnp.float32)).astype(jnp.bfloat16)
    up_ref[0] = (d_hidden * active_ref[0].astype(jnp.float32)).astype(jnp.bfloat16)


def on_tokens(name, kernel, prefetch, first, count, parts, blocks, outputs):
    features = parts[0].shape[1]
    n, width = len(blocks), blocks[0].shape[-1]
    each = pl.BlockSpec((1, count, width), lambda r, info: (r, 0, 0))
    return pl.pallas_call(
        functools.partial(kernel, n),
        grid_spec=pltpu.PrefetchScalarGridSpec(
            num_scalar_prefetch=1,
            grid=(shares,),
            in_specs=[each] * len(first) + [anywhere] * (shares + n),
            out_specs=[each] * outputs,
            scratch_shapes=[
                pltpu.VMEM((shares, *parts[0].shape), jnp.bfloat16),
                pltpu.VMEM((*blocks[0].shape[:-2], features, width), jnp.bfloat16),
                pltpu.SemaphoreType.DMA((shares,)),
                pltpu.SemaphoreType.DMA((n,)),
            ],
        ),
        out_shape=[jax.ShapeDtypeStruct((shares, count, width), jnp.bfloat16)] * outputs,
        compiler_params=params,
        cost_estimate=pl.CostEstimate(
            flops=2 * shares * count * n * blocks[0].size,
            bytes_accessed=2 * shares * count * features + 2 * n * blocks[0].size,
            transcendentals=0,
        ),
        name=name,
    )(prefetch, *first, *far_off(parts), *far_off(blocks))


def forward(info, count, x_parts, blocks):
    return on_tokens("forward", forward_kernel, info, [], count, x_parts, blocks, 3)


def grow(info, count, u_parts, blocks, factors):
    return on_tokens("grow", grow_kernel, info, factors, count, u_parts, blocks, 2)


def produce_kernel(keys, me_ref, ids_ref, hidden_ref, *refs):
    keep_ref, send_ref, down, sems = refs[len(keys) :]
    chunk, part = pl.program_id(0), pl.program_id(1)

    @pl.when(part == 0)
    def _():
        for start in (True, False):
            fetch(keys, refs[: len(keys)], me_ref[0], ids_ref[chunk], down.shape[0], down, sems, start)

    count, width = hidden_ref.shape[1:]
    produced = dot(hidden_ref[...].reshape(2 * count, width), down[...], high).astype(jnp.bfloat16)
    keep_ref[0, 0] = produced[:count]
    send_ref[0, 0] = produced[count:]


def produce(me, ids, chunks, hidden, keys, blocks, features):
    _, count, width = hidden.shape
    columns, size = features // chunks, ids.shape[0]
    half = pl.BlockSpec((1, 1, count, columns), lambda c, r, me, ids: (c, r, 0, 0))
    return pl.pallas_call(
        functools.partial(produce_kernel, keys),
        grid_spec=pltpu.PrefetchScalarGridSpec(
            num_scalar_prefetch=2,
            grid=(size, shares // 2),
            in_specs=[pl.BlockSpec((2, count, width), lambda c, r, me, ids: (r, 0, 0))] + [anywhere] * len(blocks),
            out_specs=[half, half],
            scratch_shapes=[pltpu.VMEM((columns, width), jnp.bfloat16), pltpu.SemaphoreType.DMA((len(keys),))],
        ),
        out_shape=[pltpu.HBM((size, shares // 2, count, columns), jnp.bfloat16)] * 2,
        compiler_params=params,
        cost_estimate=pl.CostEstimate(
            flops=2 * hidden.size * columns * size,
            bytes_accessed=2 * hidden.size * (size + 1),
            transcendentals=0,
        ),
        name="produce",
    )(me, ids, hidden, *far_off(blocks))


def back_kernel(n, me_ref, ids_ref, pre_ref, up_ref, *refs):
    block_refs = refs[:n]
    keep_ref, send_ref, weights, sems = refs[n:]
    chunk, part = pl.program_id(0), pl.program_id(1)
    size, span = weights.shape[0], weights.shape[2]

    for c in range(size):

        @pl.when((chunk == 0) & (part == 0))
        def _(c=c):
            fetch(range(n), block_refs, me_ref[0], ids_ref[c], span, weights.at[c], sems.at[c], True)

    for c in range(size):

        @pl.when((chunk == c) & (part == 0))
        def _(c=c):
            fetch(range(n), block_refs, me_ref[0], ids_ref[c], span, weights.at[c], sems.at[c], False)

    count, width = pre_ref.shape[1:]
    grown = dot(pre_ref[...].reshape(2 * count, width), weights[chunk, 0], high)
    grown = grown + dot(up_ref[...].reshape(2 * count, width), weights[chunk, 1], high)
    keep_ref[0, 0] = grown[:count].astype(jnp.bfloat16)
    send_ref[0, 0] = grown[count:].astype(jnp.bfloat16)


def back(me, ids, chunks, d_pre, d_up, blocks):
    _, count, width = d_pre.shape
    n, size = len(blocks), ids.shape[0]
    columns = n * blocks[0].shape[1] // chunks
    part = pl.BlockSpec((2, count, width), lambda c, r, me, ids: (r, 0, 0))
    half = pl.BlockSpec((1, 1, count, columns), lambda c, r, me, ids: (c, r, 0, 0))
    return pl.pallas_call(
        functools.partial(back_kernel, n),
        grid_spec=pltpu.PrefetchScalarGridSpec(
            num_scalar_prefetch=2,
            grid=(size, shares // 2),
            in_specs=[part, part] + [anywhere] * n,
            out_specs=[half, half],
            scratch_shapes=[
                pltpu.VMEM((size, 2, columns, width), jnp.bfloat16),
                pltpu.SemaphoreType.DMA((size, n)),
            ],
        ),
        out_shape=[pltpu.HBM((size, shares // 2, count, columns), jnp.bfloat16)] * 2,
        compiler_params=params,
        cost_estimate=pl.CostEstimate(
            flops=4 * size * shares * count * width * columns,
            bytes_accessed=4 * d_pre.size + 4 * size * columns * width,
            transcendentals=0,
        ),
        name="back",
    )(me, ids, d_pre, d_up, *far_off(blocks))


def pack_kernel(value_ref, scale_ref, tick_ref, out_ref):
    count, (experts, tokens) = value_ref.shape[0], scale_ref.shape
    out_ref[:count] = value_ref[...]
    if out_ref.shape[0] > count:
        out_ref[count:] = jnp.zeros((out_ref.shape[0] - count, out_ref.shape[1]), out_ref.dtype)
        for expert in range(experts):
            out_ref[pl.ds(count, 16), pl.ds(expert * tokens, tokens)] = jnp.broadcast_to(
                scale_ref[pl.ds(expert, 1), :], (16, tokens)
            ).astype(out_ref.dtype)


def pack(value, scale, tick, extra):
    return pl.pallas_call(
        pack_kernel,
        in_specs=[pl.BlockSpec(memory_space=pltpu.VMEM)] * 2 + [anywhere],
        out_specs=pl.BlockSpec(memory_space=pltpu.VMEM),
        out_shape=jax.ShapeDtypeStruct((value.shape[0] + extra, value.shape[1]), value.dtype),
        compiler_params=params,
        name="pack",
    )(value, scale, tick)


def token_scales(slot_token, slot_gate, block_expert, experts, token_count):
    block_rows = slot_token.shape[0] // block_expert.shape[0]
    scale = slot_gate.astype(jnp.float32) / gate_steps
    slot_expert = jnp.repeat(block_expert, block_rows)
    weight = jnp.where(slot_expert[None, :] == jnp.arange(experts)[:, None], scale[None, :], 0.0)
    hot = (slot_token[:, None] == jnp.arange(token_count)[None, :]).astype(jnp.bfloat16)
    return jnp.dot(weight.astype(jnp.bfloat16), hot, preferred_element_type=jnp.float32)


def shards(n, m, tokens, cotangent, w_gate, w_up, w_down, slot_token, slot_gate, block_expert):
    experts = w_gate.shape[0]
    count, features = tokens.shape
    columns = features // m
    me, z = lax.axis_index("dp"), lax.axis_index("etp")
    top, chip, here = n // 2, me // 2, me.reshape(1)
    gather_bits = [1 << i for i in range(1, n.bit_length() - 2)]
    single = len(gather_bits) == 1
    mine = (me & 1) + 2 * (me // top)
    pick = jnp.stack([mine ^ share for share in range(shares)]).astype(jnp.int32)
    clock = Clock()
    wide = functools.partial(jnp.asarray, dtype=jnp.float32)

    def shift(value, step):
        return lax.ppermute(value, "etp", [(i, (i + step) % m) for i in range(m)])

    have, starts, needs = {}, {}, {}
    scale = token_scales(slot_token, slot_gate, block_expert, experts, count)

    def plan(slot, until, name, source, mask):
        starts.setdefault(slot, []).append((name, source, mask))
        needs.setdefault(until, []).append(name)

    plan(0, 1, ("rows", 1), ("rows piece", 1), 1)
    plan(0, 2, ("rows", top), ("rows piece", 2), top)
    plan(1, 3, ("rows", top + 1), ("rows piece", 3), top + 1)
    plan(1, 2, ("turned", 1), ("turned piece", 1), 1)
    plan(2, 3, ("turned", top), ("turned piece", 2), top)
    plan(3, 5, "x far", "x", top)
    plan(3, 5, "x near", "x", 1)
    plan(3, 5, ("turned", top + 1), ("turned piece", 3), top + 1)
    plan(5, 6, "x far near", "x far", 1)
    plan(6, 8, "u far", "u", top)
    plan(6, 8, "u near", "u", 1)
    plan(8, 9, "u far near", "u far", 1)
    slots = [(0, 2), (1, 3), (2, 4), (3, 5), (4, 5), (5, 7), (5, 7), (6, 8)]
    moves = 0
    for kind in ("rows", "turned"):
        held = [0, 1, top, top + 1]
        for bit in gather_bits:
            for key in list(held):
                begin, until = slots[moves] if single else (moves + 3, moves + 5)
                plan(begin, until, (kind, key ^ bit), (kind, key), bit)
                held.append(key ^ bit)
                moves += 1

    def tick(at, extra=()):
        begin = starts.get(at, [])
        names = list(dict.fromkeys(source for _, source, _ in begin))
        wait = [have[name] for name in needs.get(at, [])]
        have.update(zip(names, clock.tick([have[name] for name in names], [*wait, *extra])))
        for name, source, mask in begin:
            have[name] = swap(have[source], mask, n)

    pieces = cast_rows(pick, w_gate, w_up)
    have["rows", 0] = pieces[0]
    have.update({("rows piece", share): pieces[share] for share in range(1, shares)})
    tick(0)
    pieces = cast_turned(pick, w_down, clock.token)
    have["turned", 0] = pieces[0]
    have.update({("turned piece", share): pieces[share] for share in range(1, shares)})
    tick(1)
    have["x"] = pack(tokens, scale, clock.token, 16)
    tick(2)
    have["u"] = pack(cotangent, scale, clock.token, 0)
    last = max(needs)
    halves = n == 2 * m and single
    for at in range(3, 7 if halves else last + 1):
        tick(at)

    def hold(values, *wait):
        (first,) = clock.tick(values[:1], wait)
        return [first, *values[1:]]

    blocks = hold([have["rows", key] for key in range(n)])
    info = jnp.stack([me, mine // (shares // experts)]).astype(jnp.int32)
    hidden, *factors = forward(info, count, [have[k] for k in ("x", "x near", "x far", "x far near")], blocks)

    def run(keys, ids, hidden):
        return produce(here, ids, m, hidden, keys, [have["turned", key] for key in keys], features)

    def add(keep, near):
        return (wide(keep[:, 1]) + wide(near[:, 1])).astype(jnp.bfloat16), wide(keep[:, 0]) + wide(near[:, 0])

    order = [m // 2] + [step for step in range(1, m) if step != m // 2] + [0]

    if halves:
        bit = gather_bits[0]
        first, second = [0, top], [bit, bit ^ top]
        tick(7, [hidden])
        keep_a, send_a = run([0, 1, top, top + 1], jnp.stack([chip ^ (key // 2) for key in first]), hidden)
        (send_a,) = clock.tick([send_a])
        near_a = swap(send_a, 1, n)
        clock.tick([], [have["u far"], have["turned", top + 1 + bit]])
        tick(8)
        clock.tick([], [near_a])
        other, own_a = add(keep_a, near_a)
        (other,) = clock.tick([other])
        far_a = swap(other, top, n)
        keys = [bit, bit + 1, bit + top, bit + top + 1]
        have["turned", bit] = hold([have["turned", bit]])[0]
        keep, send = run(keys, jnp.stack([chip ^ (key // 2) for key in second]), hidden)
        (send,) = clock.tick([send])
        near = swap(send, 1, n)
        tick(9)
    else:
        keep, send = run(list(range(n)), jnp.arange(m, dtype=jnp.int32), hidden)
        near = swap(send, 1, n)
    clock.tick([], [near])
    other, own = add(keep, near)
    (other,) = clock.tick([other])
    got = swap(other, top, n)
    u_parts = hold([have[name] for name in ("u", "u near", "u far", "u far near")])
    d_pre, d_up = grow(info, count, u_parts, [have["turned", key] for key in range(n)], factors)
    steps = jnp.array([order[: m // 2], order[m // 2 :]], jnp.int32)
    blocks = hold(blocks, d_pre)
    keep_0, send_0 = back(here, lax.rem(z + steps[0], m), m, d_pre, d_up, blocks)
    (send_0,) = clock.tick([send_0], [far_a, got] if halves else [got])
    near_0 = swap(send_0, 1, n)
    if halves:
        sums = [own_a[0] + wide(far_a[1]), own_a[1] + wide(far_a[0]), own[0] + wide(got[1]), own[1] + wide(got[0])]
        where = [chip ^ (key // 2) for key in first + second]
    else:
        sums = list(own + wide(got))
        where = list(range(m))

    def chunk_of(target, values):
        chosen = values[-1]
        for value, place in zip(values[:-1], where):
            chosen = jnp.where(target == place, value, chosen)
        return chosen

    combined = chunk_of(z, sums)
    low_sums = [value.astype(jnp.bfloat16) for value in sums]
    values = clock.tick([chunk_of(lax.rem(z + step, m), low_sums) for step in order[:-1]])
    late = [shift(value, step) for value, step in zip(values, order)]
    clock.tick([], [near_0])
    other, own_0 = add(keep_0, near_0)
    (other,) = clock.tick([other])
    got_0 = swap(other, top, n)
    blocks = hold(blocks)
    keep_1, send_1 = back(here, lax.rem(z + steps[1], m), m, d_pre, d_up, blocks)
    (send_1,) = clock.tick([send_1], [got_0, *late])
    near_1 = swap(send_1, 1, n)
    clock.tick([], [near_1])
    other, own_1 = add(keep_1, near_1)
    (other,) = clock.tick([other])
    got_1 = swap(other, top, n)
    for value in late:
        combined = combined + wide(value)
    owns, gots = [own_0, own_1], [got_0, got_1]
    grad = 0.0
    for i, step in enumerate(order):
        half, at = divmod(i, m // 2)
        value = owns[half][at] + wide(gots[half][at])
        if step:
            (value,) = clock.tick([value.astype(jnp.bfloat16)])
            value = wide(shift(value, step))
        grad = grad + value
    return combined.astype(jnp.bfloat16), grad.astype(jnp.bfloat16)


def solution(mesh):
    in_specs = (
        P("dp", None),
        P("dp", None),
        P(None, "dp", "etp"),
        P(None, "dp", "etp"),
        P(None, "etp", "dp"),
        P("dp"),
        P("dp"),
        P("dp"),
    )
    out_specs = (P("dp", "etp"), P("dp", "etp"))
    body = functools.partial(shards, mesh.shape["dp"], mesh.shape["etp"])
    return jax.shard_map(body, mesh=mesh, in_specs=in_specs, out_specs=out_specs, check_vma=False)
```

```python
import functools

import jax
import jax.numpy as jnp
from jax import lax
from jax.experimental import pallas as pl
from jax.experimental.pallas import tpu as pltpu
from jax.sharding import PartitionSpec as P

gate_steps = 16.0
vmem_limit = 48 * 1024 * 1024
shares = 4
slot_us = 5.0
flop_rate = 1_150_000_000
low, high = (((1,), (0,)), ((), ())), (((1,), (1,)), ((), ()))
dot = functools.partial(lax.dot_general, preferred_element_type=jnp.float32)
params = pltpu.CompilerParams(vmem_limit_bytes=vmem_limit)
anywhere = pl.BlockSpec(memory_space=pl.ANY)


def shape_of(value):
    return jax.ShapeDtypeStruct(value.shape, value.dtype)


class Clock:
    def __init__(self):
        self.token = blank((16, 128))

    def tick(self, release, wait=()):
        held = [self.token, *release]
        known = {id(value) for value in held}
        wait = [value for value in wait if id(value) not in known]
        self.token, *out = pl.pallas_call(
            lambda *refs: None,
            in_specs=[anywhere] * (len(held) + len(wait)),
            out_specs=[anywhere] * len(held),
            out_shape=[shape_of(value) for value in held],
            input_output_aliases={i: i for i in range(len(held))},
            cost_estimate=pl.CostEstimate(flops=int(slot_us * flop_rate), bytes_accessed=0, transcendentals=0),
            name="tick",
        )(*held, *wait)
        return out


def far_off(values):
    return [pltpu.with_memory_space_constraint(value, pltpu.HBM) for value in values]


def blank(shape):
    return pl.pallas_call(
        lambda *refs: None,
        out_specs=anywhere,
        out_shape=jax.ShapeDtypeStruct(shape, jnp.bfloat16),
        name="blank",
    )()


def swap(value, mask, size):
    return lax.ppermute(value, "dp", [(i, i ^ mask) for i in range(size)])


def steps_of(rows):
    return max(step for step in (1, 2, 4) if rows % (16 * step) == 0)


def cast_rows_kernel(pick_ref, gate_ref, up_ref, *out_refs):
    parts = shares // gate_ref.shape[0]
    width = out_refs[0].shape[-1]
    for share, out_ref in enumerate(out_refs):
        expert = pick_ref[share] // parts
        lanes = pl.ds(pl.multiple_of(pick_ref[share] % parts * width, 128), width)
        out_ref[0] = gate_ref[expert, :, lanes].astype(jnp.bfloat16)
        out_ref[1] = up_ref[expert, :, lanes].astype(jnp.bfloat16)


def cast_rows(pick, w_gate, w_up):
    experts, rows, hidden = w_gate.shape
    width = experts * hidden // shares
    steps = steps_of(rows)
    block = pl.BlockSpec((experts, rows // steps, hidden), lambda i, pick: (0, i, 0))
    return pl.pallas_call(
        cast_rows_kernel,
        grid_spec=pltpu.PrefetchScalarGridSpec(
            num_scalar_prefetch=1,
            grid=(steps,),
            in_specs=[block, block],
            out_specs=[pl.BlockSpec((2, rows // steps, width), lambda i, pick: (0, i, 0))] * shares,
        ),
        out_shape=[pltpu.HBM((2, rows, width), jnp.bfloat16)] * shares,
        compiler_params=params,
        name="cast_rows",
    )(pick, w_gate, w_up)


def cast_turned_kernel(pick_ref, down_ref, *refs):
    out_refs = refs[-shares:]
    parts = shares // down_ref.shape[0]
    width = out_refs[0].shape[-1]
    for share, out_ref in enumerate(out_refs):
        expert = pick_ref[share] // parts
        rows = pl.ds(pl.multiple_of(pick_ref[share] % parts * width, 128), width)
        out_ref[...] = down_ref[expert, rows, :].T.astype(jnp.bfloat16)


def cast_turned(pick, w_down, *earlier):
    experts, hidden, features = w_down.shape
    width = experts * hidden // shares
    tile = 128 if features % 128 == 0 else features
    return pl.pallas_call(
        cast_turned_kernel,
        grid_spec=pltpu.PrefetchScalarGridSpec(
            num_scalar_prefetch=1,
            grid=(features // tile,),
            in_specs=[pl.BlockSpec((experts, hidden, tile), lambda i, pick: (0, 0, i))]
            + [anywhere] * len(earlier),
            out_specs=[pl.BlockSpec((tile, width), lambda i, pick: (i, 0))] * shares,
        ),
        out_shape=[pltpu.HBM((features, width), jnp.bfloat16)] * shares,
        compiler_params=params,
        name="cast_turned",
    )(pick, w_down, *earlier)


def fetch(keys, refs, me, chunk, span, target, sems, start):
    rows = refs[0].shape[-2]
    per = span // rows
    for i, (key, ref) in enumerate(zip(keys, refs)):
        block = me ^ key

        @pl.when(block // per == chunk)
        def _(ref=ref, i=i, block=block):
            place = pl.ds(pl.multiple_of(block % per * rows, 16), rows)
            view = target.at[place] if len(target.shape) == 2 else target.at[:, place]
            copy = pltpu.make_async_copy(ref, view, sems.at[i])
            if start:
                copy.start()
            else:
                copy.wait()


def load(n, me, parts, blocks, x, weights, x_sems, sems):
    step = pl.program_id(0)
    copies = [pltpu.make_async_copy(part, x.at[i], x_sems.at[i]) for i, part in enumerate(parts)]

    @pl.when(step == 0)
    def _():
        fetch(range(n), blocks, me, 0, weights.shape[-2], weights, sems, True)
        for copy in copies:
            copy.start()
        fetch(range(n), blocks, me, 0, weights.shape[-2], weights, sems, False)

    for i, copy in enumerate(copies):

        @pl.when(step == i)
        def _(copy=copy):
            copy.wait()


def forward_kernel(n, info_ref, *refs):
    hidden_ref, pre_ref, up_ref, x, weights, x_sems, sems = refs[shares + n :]
    load(n, info_ref[0], refs[:shares], refs[shares : shares + n], x, weights, x_sems, sems)
    part = pl.program_id(0)
    inputs = x[part, : hidden_ref.shape[1]]
    gate_pre = dot(inputs, weights[0], low)
    up_pre = dot(inputs, weights[1], low)
    count = hidden_ref.shape[1]
    square = lax.broadcasted_iota(jnp.int32, (count, count), 0) == lax.broadcasted_iota(jnp.int32, (count, count), 1)
    row = x[part, pl.ds(count, 1), pl.ds(pl.multiple_of(info_ref[1] * count, 128), count)].astype(jnp.float32)
    scale = jnp.sum(jnp.where(square, row, 0.0), axis=1, keepdims=True)
    squash = 1.0 / (1.0 + jnp.exp(-gate_pre))
    active = gate_pre * squash * scale
    hidden_ref[0] = (active * up_pre).astype(jnp.bfloat16)
    slope = up_pre * squash * (1.0 + gate_pre * (1.0 - squash)) * scale
    pre_ref[0] = slope.astype(jnp.bfloat16)
    up_ref[0] = active.astype(jnp.bfloat16)


def grow_kernel(n, me_ref, slope_ref, active_ref, *refs):
    pre_ref, up_ref, u, weights, u_sems, sems = refs[shares + n :]
    load(n, me_ref[0], refs[:shares], refs[shares : shares + n], u, weights, u_sems, sems)
    d_hidden = dot(u[pl.program_id(0)], weights[...], low)
    pre_ref[0] = (d_hidden * slope_ref[0].astype(jnp.float32)).astype(jnp.bfloat16)
    up_ref[0] = (d_hidden * active_ref[0].astype(jnp.float32)).astype(jnp.bfloat16)


def on_tokens(name, kernel, prefetch, first, count, parts, blocks, outputs):
    features = parts[0].shape[1]
    n, width = len(blocks), blocks[0].shape[-1]
    each = pl.BlockSpec((1, count, width), lambda r, info: (r, 0, 0))
    return pl.pallas_call(
        functools.partial(kernel, n),
        grid_spec=pltpu.PrefetchScalarGridSpec(
            num_scalar_prefetch=1,
            grid=(shares,),
            in_specs=[each] * len(first) + [anywhere] * (shares + n),
            out_specs=[each] * outputs,
            scratch_shapes=[
                pltpu.VMEM((shares, *parts[0].shape), jnp.bfloat16),
                pltpu.VMEM((*blocks[0].shape[:-2], features, width), jnp.bfloat16),
                pltpu.SemaphoreType.DMA((shares,)),
                pltpu.SemaphoreType.DMA((n,)),
            ],
        ),
        out_shape=[jax.ShapeDtypeStruct((shares, count, width), jnp.bfloat16)] * outputs,
        compiler_params=params,
        cost_estimate=pl.CostEstimate(
            flops=2 * shares * count * n * blocks[0].size,
            bytes_accessed=2 * shares * count * features + 2 * n * blocks[0].size,
            transcendentals=0,
        ),
        name=name,
    )(prefetch, *first, *far_off(parts), *far_off(blocks))


def forward(info, count, x_parts, blocks):
    return on_tokens("forward", forward_kernel, info, [], count, x_parts, blocks, 3)


def grow(info, count, u_parts, blocks, factors):
    return on_tokens("grow", grow_kernel, info, factors, count, u_parts, blocks, 2)


def produce_kernel(keys, me_ref, ids_ref, hidden_ref, *refs):
    keep_ref, send_ref, down, sems = refs[len(keys) :]
    chunk, part = pl.program_id(0), pl.program_id(1)

    @pl.when(part == 0)
    def _():
        for start in (True, False):
            fetch(keys, refs[: len(keys)], me_ref[0], ids_ref[chunk], down.shape[0], down, sems, start)

    count, width = hidden_ref.shape[1:]
    produced = dot(hidden_ref[...].reshape(2 * count, width), down[...], high).astype(jnp.bfloat16)
    keep_ref[0, 0] = produced[:count]
    send_ref[0, 0] = produced[count:]


def produce(me, ids, chunks, hidden, keys, blocks, features):
    _, count, width = hidden.shape
    columns, size = features // chunks, ids.shape[0]
    half = pl.BlockSpec((1, 1, count, columns), lambda c, r, me, ids: (c, r, 0, 0))
    return pl.pallas_call(
        functools.partial(produce_kernel, keys),
        grid_spec=pltpu.PrefetchScalarGridSpec(
            num_scalar_prefetch=2,
            grid=(size, shares // 2),
            in_specs=[pl.BlockSpec((2, count, width), lambda c, r, me, ids: (r, 0, 0))] + [anywhere] * len(blocks),
            out_specs=[half, half],
            scratch_shapes=[pltpu.VMEM((columns, width), jnp.bfloat16), pltpu.SemaphoreType.DMA((len(keys),))],
        ),
        out_shape=[pltpu.HBM((size, shares // 2, count, columns), jnp.bfloat16)] * 2,
        compiler_params=params,
        cost_estimate=pl.CostEstimate(
            flops=2 * hidden.size * columns * size,
            bytes_accessed=2 * hidden.size * (size + 1),
            transcendentals=0,
        ),
        name="produce",
    )(me, ids, hidden, *far_off(blocks))


def back_kernel(n, me_ref, ids_ref, pre_ref, up_ref, *refs):
    block_refs = refs[:n]
    keep_ref, send_ref, weights, sems = refs[n:]
    chunk, part = pl.program_id(0), pl.program_id(1)
    size, span = weights.shape[0], weights.shape[2]

    for c in range(size):

        @pl.when((chunk == 0) & (part == 0))
        def _(c=c):
            fetch(range(n), block_refs, me_ref[0], ids_ref[c], span, weights.at[c], sems.at[c], True)

    for c in range(size):

        @pl.when((chunk == c) & (part == 0))
        def _(c=c):
            fetch(range(n), block_refs, me_ref[0], ids_ref[c], span, weights.at[c], sems.at[c], False)

    count, width = pre_ref.shape[1:]
    grown = dot(pre_ref[...].reshape(2 * count, width), weights[chunk, 0], high)
    grown = grown + dot(up_ref[...].reshape(2 * count, width), weights[chunk, 1], high)
    keep_ref[0, 0] = grown[:count].astype(jnp.bfloat16)
    send_ref[0, 0] = grown[count:].astype(jnp.bfloat16)


def back(me, ids, chunks, d_pre, d_up, blocks):
    _, count, width = d_pre.shape
    n, size = len(blocks), ids.shape[0]
    columns = n * blocks[0].shape[1] // chunks
    part = pl.BlockSpec((2, count, width), lambda c, r, me, ids: (r, 0, 0))
    half = pl.BlockSpec((1, 1, count, columns), lambda c, r, me, ids: (c, r, 0, 0))
    return pl.pallas_call(
        functools.partial(back_kernel, n),
        grid_spec=pltpu.PrefetchScalarGridSpec(
            num_scalar_prefetch=2,
            grid=(size, shares // 2),
            in_specs=[part, part] + [anywhere] * n,
            out_specs=[half, half],
            scratch_shapes=[
                pltpu.VMEM((size, 2, columns, width), jnp.bfloat16),
                pltpu.SemaphoreType.DMA((size, n)),
            ],
        ),
        out_shape=[pltpu.HBM((size, shares // 2, count, columns), jnp.bfloat16)] * 2,
        compiler_params=params,
        cost_estimate=pl.CostEstimate(
            flops=4 * size * shares * count * width * columns,
            bytes_accessed=4 * d_pre.size + 4 * size * columns * width,
            transcendentals=0,
        ),
        name="back",
    )(me, ids, d_pre, d_up, *far_off(blocks))


def pack_kernel(value_ref, scale_ref, tick_ref, out_ref):
    count, (experts, tokens) = value_ref.shape[0], scale_ref.shape
    out_ref[:count] = value_ref[...]
    if out_ref.shape[0] > count:
        out_ref[count:] = jnp.zeros((out_ref.shape[0] - count, out_ref.shape[1]), out_ref.dtype)
        for expert in range(experts):
            out_ref[pl.ds(count, 16), pl.ds(expert * tokens, tokens)] = jnp.broadcast_to(
                scale_ref[pl.ds(expert, 1), :], (16, tokens)
            ).astype(out_ref.dtype)


def pack(value, scale, tick, extra):
    return pl.pallas_call(
        pack_kernel,
        in_specs=[pl.BlockSpec(memory_space=pltpu.VMEM)] * 2 + [anywhere],
        out_specs=pl.BlockSpec(memory_space=pltpu.VMEM),
        out_shape=jax.ShapeDtypeStruct((value.shape[0] + extra, value.shape[1]), value.dtype),
        compiler_params=params,
        name="pack",
    )(value, scale, tick)


def token_scales(slot_token, slot_gate, block_expert, experts, token_count):
    block_rows = slot_token.shape[0] // block_expert.shape[0]
    scale = slot_gate.astype(jnp.float32) / gate_steps
    slot_expert = jnp.repeat(block_expert, block_rows)
    weight = jnp.where(slot_expert[None, :] == jnp.arange(experts)[:, None], scale[None, :], 0.0)
    hot = (slot_token[:, None] == jnp.arange(token_count)[None, :]).astype(jnp.bfloat16)
    return jnp.dot(weight.astype(jnp.bfloat16), hot, preferred_element_type=jnp.float32)


def shards(n, m, tokens, cotangent, w_gate, w_up, w_down, slot_token, slot_gate, block_expert):
    experts = w_gate.shape[0]
    count, features = tokens.shape
    columns = features // m
    me, z = lax.axis_index("dp"), lax.axis_index("etp")
    top, chip, here = n // 2, me // 2, me.reshape(1)
    gather_bits = [1 << i for i in range(1, n.bit_length() - 2)]
    single = len(gather_bits) == 1
    mine = (me & 1) + 2 * (me // top)
    pick = jnp.stack([mine ^ share for share in range(shares)]).astype(jnp.int32)
    clock = Clock()
    wide = functools.partial(jnp.asarray, dtype=jnp.float32)

    def shift(value, step):
        return lax.ppermute(value, "etp", [(i, (i + step) % m) for i in range(m)])

    have, starts, needs = {}, {}, {}
    scale = token_scales(slot_token, slot_gate, block_expert, experts, count)

    def plan(slot, until, name, source, mask):
        starts.setdefault(slot, []).append((name, source, mask))
        needs.setdefault(until, []).append(name)

    plan(0, 1, ("rows", 1), ("rows piece", 1), 1)
    plan(0, 2, ("rows", top), ("rows piece", 2), top)
    plan(1, 3, ("rows", top + 1), ("rows piece", 3), top + 1)
    plan(1, 2, ("turned", 1), ("turned piece", 1), 1)
    plan(2, 3, ("turned", top), ("turned piece", 2), top)
    plan(3, 5, "x far", "x", top)
    plan(3, 5, "x near", "x", 1)
    plan(3, 5, ("turned", top + 1), ("turned piece", 3), top + 1)
    plan(5, 6, "x far near", "x far", 1)
    plan(6, 8, "u far", "u", top)
    plan(6, 8, "u near", "u", 1)
    plan(8, 9, "u far near", "u far", 1)
    slots = [(0, 2), (1, 3), (2, 4), (3, 5), (4, 5), (5, 7), (5, 7), (6, 8)]
    moves = 0
    for kind in ("rows", "turned"):
        held = [0, 1, top, top + 1]
        for bit in gather_bits:
            for key in list(held):
                begin, until = slots[moves] if single else (moves + 3, moves + 5)
                plan(begin, until, (kind, key ^ bit), (kind, key), bit)
                held.append(key ^ bit)
                moves += 1

    def tick(at, extra=()):
        begin = starts.get(at, [])
        names = list(dict.fromkeys(source for _, source, _ in begin))
        wait = [have[name] for name in needs.get(at, [])]
        have.update(zip(names, clock.tick([have[name] for name in names], [*wait, *extra])))
        for name, source, mask in begin:
            have[name] = swap(have[source], mask, n)

    pieces = cast_rows(pick, w_gate, w_up)
    have["rows", 0] = pieces[0]
    have.update({("rows piece", share): pieces[share] for share in range(1, shares)})
    tick(0)
    pieces = cast_turned(pick, w_down, clock.token)
    have["turned", 0] = pieces[0]
    have.update({("turned piece", share): pieces[share] for share in range(1, shares)})
    tick(1)
    have["x"] = pack(tokens, scale, clock.token, 16)
    tick(2)
    have["u"] = pack(cotangent, scale, clock.token, 0)
    last = max(needs)
    halves = n == 2 * m and single
    for at in range(3, 7 if halves else last + 1):
        tick(at)

    def hold(values, *wait):
        (first,) = clock.tick(values[:1], wait)
        return [first, *values[1:]]

    blocks = hold([have["rows", key] for key in range(n)])
    info = jnp.stack([me, mine // (shares // experts)]).astype(jnp.int32)
    hidden, *factors = forward(info, count, [have[k] for k in ("x", "x near", "x far", "x far near")], blocks)

    def run(keys, ids, hidden):
        return produce(here, ids, m, hidden, keys, [have["turned", key] for key in keys], features)

    def add(keep, near):
        return (wide(keep[:, 1]) + wide(near[:, 1])).astype(jnp.bfloat16), wide(keep[:, 0]) + wide(near[:, 0])

    order = [m // 2] + [step for step in range(1, m) if step != m // 2] + [0]

    if halves:
        bit = gather_bits[0]
        first, second = [0, top], [bit, bit ^ top]
        tick(7, [hidden])
        keep_a, send_a = run([0, 1, top, top + 1], jnp.stack([chip ^ (key // 2) for key in first]), hidden)
        (send_a,) = clock.tick([send_a])
        near_a = swap(send_a, 1, n)
        clock.tick([], [have["u far"], have["turned", top + 1 + bit]])
        tick(8)
        clock.tick([], [near_a])
        other, own_a = add(keep_a, near_a)
        (other,) = clock.tick([other])
        far_a = swap(other, top, n)
        keys = [bit, bit + 1, bit + top, bit + top + 1]
        have["turned", bit] = hold([have["turned", bit]])[0]
        keep, send = run(keys, jnp.stack([chip ^ (key // 2) for key in second]), hidden)
        (send,) = clock.tick([send])
        near = swap(send, 1, n)
        tick(9)
    else:
        keep, send = run(list(range(n)), jnp.arange(m, dtype=jnp.int32), hidden)
        near = swap(send, 1, n)
    clock.tick([], [near])
    other, own = add(keep, near)
    (other,) = clock.tick([other])
    got = swap(other, top, n)
    u_parts = hold([have[name] for name in ("u", "u near", "u far", "u far near")])
    d_pre, d_up = grow(info, count, u_parts, [have["turned", key] for key in range(n)], factors)
    steps = jnp.array([order[: m // 2], order[m // 2 :]], jnp.int32)
    blocks = hold(blocks, d_pre)
    keep_0, send_0 = back(here, lax.rem(z + steps[0], m), m, d_pre, d_up, blocks)
    (send_0,) = clock.tick([send_0], [far_a, got] if halves else [got])
    near_0 = swap(send_0, 1, n)
    if halves:
        sums = [own_a[0] + wide(far_a[1]), own_a[1] + wide(far_a[0]), own[0] + wide(got[1]), own[1] + wide(got[0])]
        where = [chip ^ (key // 2) for key in first + second]
    else:
        sums = list(own + wide(got))
        where = list(range(m))

    def chunk_of(target, values):
        chosen = values[-1]
        for value, place in zip(values[:-1], where):
            chosen = jnp.where(target == place, value, chosen)
        return chosen

    combined = chunk_of(z, sums)
    low_sums = [value.astype(jnp.bfloat16) for value in sums]
    values = clock.tick([chunk_of(lax.rem(z + step, m), low_sums) for step in order[:-1]])
    late = [shift(value, step) for value, step in zip(values, order)]
    clock.tick([], [near_0])
    other, own_0 = add(keep_0, near_0)
    (other,) = clock.tick([other])
    got_0 = swap(other, top, n)
    blocks = hold(blocks)
    keep_1, send_1 = back(here, lax.rem(z + steps[1], m), m, d_pre, d_up, blocks)
    (send_1,) = clock.tick([send_1], late[1:])
    near_1 = swap(send_1, 1, n)
    clock.tick([], [got_0])
    clock.tick([], [near_1])
    other, own_1 = add(keep_1, near_1)
    (other,) = clock.tick([other])
    got_1 = swap(other, top, n)
    for value in late:
        combined = combined + wide(value)
    owns, gots = [own_0, own_1], [got_0, got_1]
    grad = 0.0
    for i, step in enumerate(order):
        half, at = divmod(i, m // 2)
        value = owns[half][at] + wide(gots[half][at])
        if step:
            (value,) = clock.tick([value.astype(jnp.bfloat16)], late[:1] if i == 0 else [])
            value = wide(shift(value, step))
        grad = grad + value
    return combined.astype(jnp.bfloat16), grad.astype(jnp.bfloat16)


def solution(mesh):
    in_specs = (
        P("dp", None),
        P("dp", None),
        P(None, "dp", "etp"),
        P(None, "dp", "etp"),
        P(None, "etp", "dp"),
        P("dp"),
        P("dp"),
        P("dp"),
    )
    out_specs = (P("dp", "etp"), P("dp", "etp"))
    body = functools.partial(shards, mesh.shape["dp"], mesh.shape["etp"])
    return jax.shard_map(body, mesh=mesh, in_specs=in_specs, out_specs=out_specs, check_vma=False)
```

```python
import functools

import jax
import jax.numpy as jnp
from jax import lax
from jax.experimental import pallas as pl
from jax.experimental.pallas import tpu as pltpu
from jax.sharding import PartitionSpec as P

gate_steps = 16.0
vmem_limit = 48 * 1024 * 1024
shares = 4
slot_us = 5.0
flop_rate = 1_150_000_000
low, high = (((1,), (0,)), ((), ())), (((1,), (1,)), ((), ()))
dot = functools.partial(lax.dot_general, preferred_element_type=jnp.float32)
params = pltpu.CompilerParams(vmem_limit_bytes=vmem_limit)
anywhere = pl.BlockSpec(memory_space=pl.ANY)


def shape_of(value):
    return jax.ShapeDtypeStruct(value.shape, value.dtype)


class Clock:
    def __init__(self):
        self.token = blank((16, 128))

    def tick(self, release, wait=()):
        held = [self.token, *release]
        known = {id(value) for value in held}
        wait = [value for value in wait if id(value) not in known]
        self.token, *out = pl.pallas_call(
            lambda *refs: None,
            in_specs=[anywhere] * (len(held) + len(wait)),
            out_specs=[anywhere] * len(held),
            out_shape=[shape_of(value) for value in held],
            input_output_aliases={i: i for i in range(len(held))},
            cost_estimate=pl.CostEstimate(flops=int(slot_us * flop_rate), bytes_accessed=0, transcendentals=0),
            name="tick",
        )(*held, *wait)
        return out


def far_off(values):
    return [pltpu.with_memory_space_constraint(value, pltpu.HBM) for value in values]


def blank(shape):
    return pl.pallas_call(
        lambda *refs: None,
        out_specs=anywhere,
        out_shape=jax.ShapeDtypeStruct(shape, jnp.bfloat16),
        name="blank",
    )()


def swap(value, mask, size):
    return lax.ppermute(value, "dp", [(i, i ^ mask) for i in range(size)])


def steps_of(rows):
    return max(step for step in (1, 2, 4) if rows % (16 * step) == 0)


def cast_rows_kernel(pick_ref, gate_ref, up_ref, *out_refs):
    parts = shares // gate_ref.shape[0]
    width = out_refs[0].shape[-1]
    for share, out_ref in enumerate(out_refs):
        expert = pick_ref[share] // parts
        lanes = pl.ds(pl.multiple_of(pick_ref[share] % parts * width, 128), width)
        out_ref[0] = gate_ref[expert, :, lanes].astype(jnp.bfloat16)
        out_ref[1] = up_ref[expert, :, lanes].astype(jnp.bfloat16)


def cast_rows(pick, w_gate, w_up):
    experts, rows, hidden = w_gate.shape
    width = experts * hidden // shares
    steps = steps_of(rows)
    block = pl.BlockSpec((experts, rows // steps, hidden), lambda i, pick: (0, i, 0))
    return pl.pallas_call(
        cast_rows_kernel,
        grid_spec=pltpu.PrefetchScalarGridSpec(
            num_scalar_prefetch=1,
            grid=(steps,),
            in_specs=[block, block],
            out_specs=[pl.BlockSpec((2, rows // steps, width), lambda i, pick: (0, i, 0))] * shares,
        ),
        out_shape=[pltpu.HBM((2, rows, width), jnp.bfloat16)] * shares,
        compiler_params=params,
        name="cast_rows",
    )(pick, w_gate, w_up)


def cast_turned_kernel(pick_ref, down_ref, *refs):
    out_refs = refs[-shares:]
    parts = shares // down_ref.shape[0]
    width = out_refs[0].shape[-1]
    for share, out_ref in enumerate(out_refs):
        expert = pick_ref[share] // parts
        rows = pl.ds(pl.multiple_of(pick_ref[share] % parts * width, 128), width)
        out_ref[...] = down_ref[expert, rows, :].T.astype(jnp.bfloat16)


def cast_turned(pick, w_down, *earlier):
    experts, hidden, features = w_down.shape
    width = experts * hidden // shares
    tile = 128 if features % 128 == 0 else features
    return pl.pallas_call(
        cast_turned_kernel,
        grid_spec=pltpu.PrefetchScalarGridSpec(
            num_scalar_prefetch=1,
            grid=(features // tile,),
            in_specs=[pl.BlockSpec((experts, hidden, tile), lambda i, pick: (0, 0, i))]
            + [anywhere] * len(earlier),
            out_specs=[pl.BlockSpec((tile, width), lambda i, pick: (i, 0))] * shares,
        ),
        out_shape=[pltpu.HBM((features, width), jnp.bfloat16)] * shares,
        compiler_params=params,
        name="cast_turned",
    )(pick, w_down, *earlier)


def fetch(keys, refs, me, chunk, span, target, sems, start):
    rows = refs[0].shape[-2]
    per = span // rows
    for i, (key, ref) in enumerate(zip(keys, refs)):
        block = me ^ key

        @pl.when(block // per == chunk)
        def _(ref=ref, i=i, block=block):
            place = pl.ds(pl.multiple_of(block % per * rows, 16), rows)
            view = target.at[place] if len(target.shape) == 2 else target.at[:, place]
            copy = pltpu.make_async_copy(ref, view, sems.at[i])
            if start:
                copy.start()
            else:
                copy.wait()


def load(n, me, parts, blocks, x, weights, x_sems, sems):
    step = pl.program_id(0)
    copies = [pltpu.make_async_copy(part, x.at[i], x_sems.at[i]) for i, part in enumerate(parts)]

    @pl.when(step == 0)
    def _():
        fetch(range(n), blocks, me, 0, weights.shape[-2], weights, sems, True)
        for copy in copies:
            copy.start()
        fetch(range(n), blocks, me, 0, weights.shape[-2], weights, sems, False)

    for i, copy in enumerate(copies):

        @pl.when(step == i)
        def _(copy=copy):
            copy.wait()


def forward_kernel(n, info_ref, *refs):
    hidden_ref, pre_ref, up_ref, x, weights, x_sems, sems = refs[shares + n :]
    load(n, info_ref[0], refs[:shares], refs[shares : shares + n], x, weights, x_sems, sems)
    part = pl.program_id(0)
    inputs = x[part, : hidden_ref.shape[1]]
    gate_pre = dot(inputs, weights[0], low)
    up_pre = dot(inputs, weights[1], low)
    count = hidden_ref.shape[1]
    square = lax.broadcasted_iota(jnp.int32, (count, count), 0) == lax.broadcasted_iota(jnp.int32, (count, count), 1)
    row = x[part, pl.ds(count, 1), pl.ds(pl.multiple_of(info_ref[1] * count, 128), count)].astype(jnp.float32)
    scale = jnp.sum(jnp.where(square, row, 0.0), axis=1, keepdims=True)
    squash = 1.0 / (1.0 + jnp.exp(-gate_pre))
    active = gate_pre * squash * scale
    hidden_ref[0] = (active * up_pre).astype(jnp.bfloat16)
    slope = up_pre * squash * (1.0 + gate_pre * (1.0 - squash)) * scale
    pre_ref[0] = slope.astype(jnp.bfloat16)
    up_ref[0] = active.astype(jnp.bfloat16)


def grow_kernel(n, me_ref, slope_ref, active_ref, *refs):
    pre_ref, up_ref, u, weights, u_sems, sems = refs[shares + n :]
    load(n, me_ref[0], refs[:shares], refs[shares : shares + n], u, weights, u_sems, sems)
    d_hidden = dot(u[pl.program_id(0)], weights[...], low)
    pre_ref[0] = (d_hidden * slope_ref[0].astype(jnp.float32)).astype(jnp.bfloat16)
    up_ref[0] = (d_hidden * active_ref[0].astype(jnp.float32)).astype(jnp.bfloat16)


def on_tokens(name, kernel, prefetch, first, count, parts, blocks, outputs):
    features = parts[0].shape[1]
    n, width = len(blocks), blocks[0].shape[-1]
    each = pl.BlockSpec((1, count, width), lambda r, info: (r, 0, 0))
    return pl.pallas_call(
        functools.partial(kernel, n),
        grid_spec=pltpu.PrefetchScalarGridSpec(
            num_scalar_prefetch=1,
            grid=(shares,),
            in_specs=[each] * len(first) + [anywhere] * (shares + n),
            out_specs=[each] * outputs,
            scratch_shapes=[
                pltpu.VMEM((shares, *parts[0].shape), jnp.bfloat16),
                pltpu.VMEM((*blocks[0].shape[:-2], features, width), jnp.bfloat16),
                pltpu.SemaphoreType.DMA((shares,)),
                pltpu.SemaphoreType.DMA((n,)),
            ],
        ),
        out_shape=[jax.ShapeDtypeStruct((shares, count, width), jnp.bfloat16)] * outputs,
        compiler_params=params,
        cost_estimate=pl.CostEstimate(
            flops=2 * shares * count * n * blocks[0].size,
            bytes_accessed=2 * shares * count * features + 2 * n * blocks[0].size,
            transcendentals=0,
        ),
        name=name,
    )(prefetch, *first, *far_off(parts), *far_off(blocks))


def forward(info, count, x_parts, blocks):
    return on_tokens("forward", forward_kernel, info, [], count, x_parts, blocks, 3)


def grow(info, count, u_parts, blocks, factors):
    return on_tokens("grow", grow_kernel, info, factors, count, u_parts, blocks, 2)


def produce_kernel(keys, me_ref, ids_ref, hidden_ref, *refs):
    keep_ref, send_ref, down, sems = refs[len(keys) :]
    chunk, part = pl.program_id(0), pl.program_id(1)

    @pl.when(part == 0)
    def _():
        for start in (True, False):
            fetch(keys, refs[: len(keys)], me_ref[0], ids_ref[chunk], down.shape[0], down, sems, start)

    count, width = hidden_ref.shape[1:]
    produced = dot(hidden_ref[...].reshape(2 * count, width), down[...], high).astype(jnp.bfloat16)
    keep_ref[0, 0] = produced[:count]
    send_ref[0, 0] = produced[count:]


def produce(me, ids, chunks, hidden, keys, blocks, features):
    _, count, width = hidden.shape
    columns, size = features // chunks, ids.shape[0]
    half = pl.BlockSpec((1, 1, count, columns), lambda c, r, me, ids: (c, r, 0, 0))
    return pl.pallas_call(
        functools.partial(produce_kernel, keys),
        grid_spec=pltpu.PrefetchScalarGridSpec(
            num_scalar_prefetch=2,
            grid=(size, shares // 2),
            in_specs=[pl.BlockSpec((2, count, width), lambda c, r, me, ids: (r, 0, 0))] + [anywhere] * len(blocks),
            out_specs=[half, half],
            scratch_shapes=[pltpu.VMEM((columns, width), jnp.bfloat16), pltpu.SemaphoreType.DMA((len(keys),))],
        ),
        out_shape=[pltpu.HBM((size, shares // 2, count, columns), jnp.bfloat16)] * 2,
        compiler_params=params,
        cost_estimate=pl.CostEstimate(
            flops=2 * hidden.size * columns * size,
            bytes_accessed=2 * hidden.size * (size + 1),
            transcendentals=0,
        ),
        name="produce",
    )(me, ids, hidden, *far_off(blocks))


def back_kernel(n, me_ref, ids_ref, pre_ref, up_ref, *refs):
    block_refs = refs[:n]
    keep_ref, send_ref, weights, sems = refs[n:]
    chunk, part = pl.program_id(0), pl.program_id(1)
    size, span = weights.shape[0], weights.shape[2]

    for c in range(size):

        @pl.when((chunk == 0) & (part == 0))
        def _(c=c):
            fetch(range(n), block_refs, me_ref[0], ids_ref[c], span, weights.at[c], sems.at[c], True)

    for c in range(size):

        @pl.when((chunk == c) & (part == 0))
        def _(c=c):
            fetch(range(n), block_refs, me_ref[0], ids_ref[c], span, weights.at[c], sems.at[c], False)

    count, width = pre_ref.shape[1:]
    grown = dot(pre_ref[...].reshape(2 * count, width), weights[chunk, 0], high)
    grown = grown + dot(up_ref[...].reshape(2 * count, width), weights[chunk, 1], high)
    keep_ref[0, 0] = grown[:count].astype(jnp.bfloat16)
    send_ref[0, 0] = grown[count:].astype(jnp.bfloat16)


def back(me, ids, chunks, d_pre, d_up, blocks):
    _, count, width = d_pre.shape
    n, size = len(blocks), ids.shape[0]
    columns = n * blocks[0].shape[1] // chunks
    part = pl.BlockSpec((2, count, width), lambda c, r, me, ids: (r, 0, 0))
    half = pl.BlockSpec((1, 1, count, columns), lambda c, r, me, ids: (c, r, 0, 0))
    return pl.pallas_call(
        functools.partial(back_kernel, n),
        grid_spec=pltpu.PrefetchScalarGridSpec(
            num_scalar_prefetch=2,
            grid=(size, shares // 2),
            in_specs=[part, part] + [anywhere] * n,
            out_specs=[half, half],
            scratch_shapes=[
                pltpu.VMEM((size, 2, columns, width), jnp.bfloat16),
                pltpu.SemaphoreType.DMA((size, n)),
            ],
        ),
        out_shape=[pltpu.HBM((size, shares // 2, count, columns), jnp.bfloat16)] * 2,
        compiler_params=params,
        cost_estimate=pl.CostEstimate(
            flops=4 * size * shares * count * width * columns,
            bytes_accessed=4 * d_pre.size + 4 * size * columns * width,
            transcendentals=0,
        ),
        name="back",
    )(me, ids, d_pre, d_up, *far_off(blocks))


def pack_kernel(value_ref, scale_ref, tick_ref, out_ref):
    count, (experts, tokens) = value_ref.shape[0], scale_ref.shape
    out_ref[:count] = value_ref[...]
    if out_ref.shape[0] > count:
        out_ref[count:] = jnp.zeros((out_ref.shape[0] - count, out_ref.shape[1]), out_ref.dtype)
        for expert in range(experts):
            out_ref[pl.ds(count, 16), pl.ds(expert * tokens, tokens)] = jnp.broadcast_to(
                scale_ref[pl.ds(expert, 1), :], (16, tokens)
            ).astype(out_ref.dtype)


def pack(value, scale, tick, extra):
    return pl.pallas_call(
        pack_kernel,
        in_specs=[pl.BlockSpec(memory_space=pltpu.VMEM)] * 2 + [anywhere],
        out_specs=pl.BlockSpec(memory_space=pltpu.VMEM),
        out_shape=jax.ShapeDtypeStruct((value.shape[0] + extra, value.shape[1]), value.dtype),
        compiler_params=params,
        name="pack",
    )(value, scale, tick)


def token_scales(slot_token, slot_gate, block_expert, experts, token_count):
    block_rows = slot_token.shape[0] // block_expert.shape[0]
    scale = slot_gate.astype(jnp.float32) / gate_steps
    slot_expert = jnp.repeat(block_expert, block_rows)
    weight = jnp.where(slot_expert[None, :] == jnp.arange(experts)[:, None], scale[None, :], 0.0)
    hot = (slot_token[:, None] == jnp.arange(token_count)[None, :]).astype(jnp.bfloat16)
    return jnp.dot(weight.astype(jnp.bfloat16), hot, preferred_element_type=jnp.float32)


def shards(n, m, tokens, cotangent, w_gate, w_up, w_down, slot_token, slot_gate, block_expert):
    experts = w_gate.shape[0]
    count, features = tokens.shape
    columns = features // m
    me, z = lax.axis_index("dp"), lax.axis_index("etp")
    top, chip, here = n // 2, me // 2, me.reshape(1)
    gather_bits = [1 << i for i in range(1, n.bit_length() - 2)]
    single = len(gather_bits) == 1
    mine = (me & 1) + 2 * (me // top)
    pick = jnp.stack([mine ^ share for share in range(shares)]).astype(jnp.int32)
    clock = Clock()
    wide = functools.partial(jnp.asarray, dtype=jnp.float32)

    def shift(value, step):
        return lax.ppermute(value, "etp", [(i, (i + step) % m) for i in range(m)])

    have, starts, needs = {}, {}, {}
    scale = token_scales(slot_token, slot_gate, block_expert, experts, count)

    def plan(slot, until, name, source, mask):
        starts.setdefault(slot, []).append((name, source, mask))
        needs.setdefault(until, []).append(name)

    plan(0, 1, ("rows", 1), ("rows piece", 1), 1)
    plan(0, 2, ("rows", top), ("rows piece", 2), top)
    plan(1, 3, ("rows", top + 1), ("rows piece", 3), top + 1)
    plan(1, 2, ("turned", 1), ("turned piece", 1), 1)
    plan(2, 3, ("turned", top), ("turned piece", 2), top)
    plan(3, 5, "x far", "x", top)
    plan(3, 5, "x near", "x", 1)
    plan(3, 5, ("turned", top + 1), ("turned piece", 3), top + 1)
    plan(5, 6, "x far near", "x far", 1)
    plan(6, 8, "u far", "u", top)
    plan(6, 8, "u near", "u", 1)
    plan(8, 9, "u far near", "u far", 1)
    slots = [(0, 2), (1, 3), (2, 4), (3, 5), (4, 5), (5, 7), (5, 7), (6, 8)]
    moves = 0
    for kind in ("rows", "turned"):
        held = [0, 1, top, top + 1]
        for bit in gather_bits:
            for key in list(held):
                begin, until = slots[moves] if single else (moves + 3, moves + 5)
                plan(begin, until, (kind, key ^ bit), (kind, key), bit)
                held.append(key ^ bit)
                moves += 1

    def tick(at, extra=()):
        begin = starts.get(at, [])
        names = list(dict.fromkeys(source for _, source, _ in begin))
        wait = [have[name] for name in needs.get(at, [])]
        have.update(zip(names, clock.tick([have[name] for name in names], [*wait, *extra])))
        for name, source, mask in begin:
            have[name] = swap(have[source], mask, n)

    pieces = cast_rows(pick, w_gate, w_up)
    have["rows", 0] = pieces[0]
    have.update({("rows piece", share): pieces[share] for share in range(1, shares)})
    tick(0)
    pieces = cast_turned(pick, w_down, clock.token)
    have["turned", 0] = pieces[0]
    have.update({("turned piece", share): pieces[share] for share in range(1, shares)})
    tick(1)
    have["x"] = pack(tokens, scale, clock.token, 16)
    tick(2)
    have["u"] = pack(cotangent, scale, clock.token, 0)
    last = max(needs)
    halves = n == 2 * m and single
    for at in range(3, 7 if halves else last + 1):
        tick(at)

    def hold(values, *wait):
        (first,) = clock.tick(values[:1], wait)
        return [first, *values[1:]]

    blocks = hold([have["rows", key] for key in range(n)])
    info = jnp.stack([me, mine // (shares // experts)]).astype(jnp.int32)
    hidden, *factors = forward(info, count, [have[k] for k in ("x", "x near", "x far", "x far near")], blocks)

    def run(keys, ids, hidden):
        return produce(here, ids, m, hidden, keys, [have["turned", key] for key in keys], features)

    def add(keep, near):
        return (wide(keep[:, 1]) + wide(near[:, 1])).astype(jnp.bfloat16), wide(keep[:, 0]) + wide(near[:, 0])

    order = [m // 2] + [step for step in range(1, m) if step != m // 2] + [0]

    if halves:
        bit = gather_bits[0]
        first, second = [0, top], [bit, bit ^ top]
        tick(7, [hidden])
        keep_a, send_a = run([0, 1, top, top + 1], jnp.stack([chip ^ (key // 2) for key in first]), hidden)
        (send_a,) = clock.tick([send_a])
        near_a = swap(send_a, 1, n)
        clock.tick([], [have["u far"], have["turned", top + 1 + bit]])
        tick(8)
        clock.tick([], [near_a])
        other, own_a = add(keep_a, near_a)
        (other,) = clock.tick([other])
        far_a = swap(other, top, n)
        keys = [bit, bit + 1, bit + top, bit + top + 1]
        have["turned", bit] = hold([have["turned", bit]])[0]
        keep, send = run(keys, jnp.stack([chip ^ (key // 2) for key in second]), hidden)
        (send,) = clock.tick([send])
        near = swap(send, 1, n)
        tick(9)
    else:
        keep, send = run(list(range(n)), jnp.arange(m, dtype=jnp.int32), hidden)
        near = swap(send, 1, n)
    clock.tick([], [near])
    other, own = add(keep, near)
    (other,) = clock.tick([other])
    got = swap(other, top, n)
    u_parts = hold([have[name] for name in ("u", "u near", "u far", "u far near")])
    d_pre, d_up = grow(info, count, u_parts, [have["turned", key] for key in range(n)], factors)
    steps = jnp.array([order[: m // 2], order[m // 2 :]], jnp.int32)
    blocks = hold(blocks)
    keep_0, send_0 = back(here, lax.rem(z + steps[0], m), m, d_pre, d_up, blocks)
    (send_0,) = clock.tick([send_0], [far_a, got] if halves else [got])
    near_0 = swap(send_0, 1, n)
    if halves:
        sums = [own_a[0] + wide(far_a[1]), own_a[1] + wide(far_a[0]), own[0] + wide(got[1]), own[1] + wide(got[0])]
        where = [chip ^ (key // 2) for key in first + second]
    else:
        sums = list(own + wide(got))
        where = list(range(m))

    def chunk_of(target, values):
        chosen = values[-1]
        for value, place in zip(values[:-1], where):
            chosen = jnp.where(target == place, value, chosen)
        return chosen

    combined = chunk_of(z, sums)
    low_sums = [value.astype(jnp.bfloat16) for value in sums]
    values = clock.tick([chunk_of(lax.rem(z + step, m), low_sums) for step in order[:-1]])
    late = [shift(value, step) for value, step in zip(values, order)]
    clock.tick([], [near_0])
    other, own_0 = add(keep_0, near_0)
    (other,) = clock.tick([other])
    got_0 = swap(other, top, n)
    blocks = hold(blocks)
    keep_1, send_1 = back(here, lax.rem(z + steps[1], m), m, d_pre, d_up, blocks)
    (send_1,) = clock.tick([send_1], late[1:])
    near_1 = swap(send_1, 1, n)
    clock.tick([], [got_0])
    clock.tick([], [near_1])
    other, own_1 = add(keep_1, near_1)
    (other,) = clock.tick([other])
    got_1 = swap(other, top, n)
    for value in late:
        combined = combined + wide(value)
    owns, gots = [own_0, own_1], [got_0, got_1]
    grad = 0.0
    for i, step in enumerate(order):
        half, at = divmod(i, m // 2)
        value = owns[half][at] + wide(gots[half][at])
        if step:
            (value,) = clock.tick([value.astype(jnp.bfloat16)], late[:1] if i == 0 else [])
            value = wide(shift(value, step))
        grad = grad + value
    return combined.astype(jnp.bfloat16), grad.astype(jnp.bfloat16)


def solution(mesh):
    in_specs = (
        P("dp", None),
        P("dp", None),
        P(None, "dp", "etp"),
        P(None, "dp", "etp"),
        P(None, "etp", "dp"),
        P("dp"),
        P("dp"),
        P("dp"),
    )
    out_specs = (P("dp", "etp"), P("dp", "etp"))
    body = functools.partial(shards, mesh.shape["dp"], mesh.shape["etp"])
    return jax.shard_map(body, mesh=mesh, in_specs=in_specs, out_specs=out_specs, check_vma=False)
```
